32 devices in a mesh: frame: 4 (over y, x), clip: 8 (over z, core).
Axes of the slice: x: 2, y: 2, z: 4, core: 2. Of those that a mesh axis runs over, the one named last changes fastest.
Arguments:
- tokens: bfloat16 [32, 1568, 384], P('clip', 'frame'), may hold values from -6 to 6
- out_grad: bfloat16 [32, 1568, 384], P('clip', 'frame'), may hold values from -6 to 6
- view_masks: int32 [32, 2, 1568], P('clip', None, 'frame'), may hold values from 0 to 1
- view_group: int32 [32, 2], P('clip'), may hold values from 0 to 1
- w_qkv: bfloat16 [384, 1152], replicated, may hold values from -0.3125 to 0.3125
- query_bias: float32 [384], replicated, may hold values from -3 to 3
- value_bias: float32 [384], replicated, may hold values from -3 to 3
- w_proj: bfloat16 [384, 384], replicated, may hold values from -2.5 to 2.5
- proj_bias: float32 [384], replicated, may hold values from -2 to 2
- w_up: bfloat16 [384, 1536], replicated, may hold values from -0.3125 to 0.3125
- up_bias: float32 [1536], replicated, may hold values from -3 to 3
- w_down: bfloat16 [1536, 384], replicated, may hold values from -0.15625 to 0.15625
- down_bias: float32 [384], replicated, may hold values from -2 to 2
- gain_one: float32 [384], replicated, may hold values from 0.25 to 1.75
- shift_one: float32 [384], replicated, may hold values from -2 to 2
- gain_two: float32 [384], replicated, may hold values from 0.25 to 1.75
- shift_two: float32 [384], replicated, may hold values from -2 to 2
Outputs:
- block_out: bfloat16 [32, 1568, 384], P('clip', 'frame')
- group_stats: float32 [32, 2, 2, 384], P('clip')
- grad_tokens: bfloat16 [32, 1568, 384], P('clip', 'frame')
- grad_w_qkv: float32 [384, 1152], replicated
- grad_query_bias: float32 [384], replicated
- grad_value_bias: float32 [384], replicated
- grad_w_proj: float32 [384, 384], replicated
- grad_proj_bias: float32 [384], replicated
- grad_w_up: float32 [384, 1536], replicated
- grad_up_bias: float32 [1536], replicated
- grad_w_down: float32 [1536, 384], replicated
- grad_down_bias: float32 [384], replicated
- grad_gain_one: float32 [384], replicated
- grad_shift_one: float32 [384], replicated
- grad_gain_two: float32 [384], replicated
- grad_shift_two: float32 [384], replicated
The draws below stay inside these ranges and needn't reach their ends.
All inputs are finite; a program needn't handle non-finite values.
Results may differ from the reference program's by a relative error of at most 0.012.
Values may be sent and summed in bfloat16 or wider, within the bound.
A program may use at most 256 MiB of HBM per device.

```python
import jax
import jax.numpy as jnp
from jax import lax

D = 384
HEADS = 6
FF = 1536
NF = 8
HW = 196
GROUPS = 2
VIEWS = 2
POS = 1568
CLIPS = 32


def draw_view_masks(key, part):
    frame_of = jnp.arange(POS, dtype=jnp.int32) // HW
    limit = 25 + 60 * frame_of // (NF - 1)
    ticket = jax.random.randint(key, (CLIPS, VIEWS, POS), 0, 100)
    return (ticket < limit[None, None, :]).astype(jnp.int32)


def with_ends(result, rng, smallest, high):
    longest = result.shape.index(max(result.shape))
    spots = []
    for shift in (0, 1):
        where = [jax.random.randint(jax.random.fold_in(rng, axis), (), 0, length) for axis, length in enumerate(result.shape)]
        where[longest] = (where[longest] + shift) % result.shape[longest]
        spots.append(tuple(where))
    return result.at[spots[0]].set(smallest).at[spots[1]].set(high)


def steps_of(stream_key, dims, pieces, smallest, largest):
    gain = 1.0
    for position, shards_of in pieces:
        draws = jax.random.uniform(jax.random.fold_in(jax.random.fold_in(stream_key, 6), position), (shards_of,), jnp.float32, smallest / len(pieces), largest / len(pieces))
        gain = gain * jnp.repeat(jnp.exp(draws), dims[position] // shards_of).reshape((-1,) + (1,) * (len(dims) - 1 - position))
    return gain


def noise(key, shape, scale, bound, cuts=(), held_as=jnp.bfloat16):
    array = jax.random.normal(key, shape, jnp.float32) * scale
    if len(cuts) > 0:
        array = steps_of(key, shape, cuts, -0.22, 0.18) * array
    return jnp.clip(array, min=-bound, max=bound).astype(held_as)


def setup_inputs(seed: int = 0) -> dict:
    key_of = jax.random.split(jax.random.key(seed), 18)
    tokens = noise(key_of[0], (CLIPS, POS, D), 1.0, 6.0, ((0, 8), (1, 4)))
    out_grad = noise(key_of[1], (CLIPS, POS, D), 1.0, 6.0, ((0, 8), (1, 4)))
    view_masks = draw_view_masks(jax.random.fold_in(key_of[17], 71), 0)
    view_group = with_ends(jax.random.randint(key_of[3], (CLIPS, VIEWS), 0, GROUPS), jax.random.fold_in(key_of[3], 1), 0, GROUPS - 1).astype(jnp.int32)
    w_qkv = noise(key_of[4], (D, 3 * D), D ** -0.5, 0.3125)
    query_bias = noise(key_of[5], (D,), 0.5, 3.0, (), jnp.float32)
    value_bias = noise(key_of[6], (D,), 0.5, 3.0, (), jnp.float32)
    w_proj = noise(key_of[7], (D, D), (D // 64) ** -0.5, 2.5)
    proj_bias = noise(key_of[8], (D,), 0.3, 2.0, (), jnp.float32)
    w_up = noise(key_of[9], (D, FF), D ** -0.5, 0.3125)
    up_bias = noise(key_of[10], (FF,), 0.5, 3.0, (), jnp.float32)
    w_down = noise(key_of[11], (FF, D), FF ** -0.5, 0.15625)
    down_bias = noise(key_of[12], (D,), 0.3, 2.0, (), jnp.float32)
    gain_one = jnp.clip(1.0 + 0.15 * jax.random.normal(key_of[13], (D,), jnp.float32), 0.25, 1.75)
    shift_one = noise(key_of[14], (D,), 0.3, 2.0, (), jnp.float32)
    gain_two = jnp.clip(1.0 + 0.15 * jax.random.normal(key_of[15], (D,), jnp.float32), 0.25, 1.75)
    shift_two = noise(key_of[16], (D,), 0.3, 2.0, (), jnp.float32)
    return dict(tokens=tokens, out_grad=out_grad, view_masks=view_masks, view_group=view_group, w_qkv=w_qkv, query_bias=query_bias, value_bias=value_bias, w_proj=w_proj, proj_bias=proj_bias, w_up=w_up, up_bias=up_bias, w_down=w_down, down_bias=down_bias, gain_one=gain_one, shift_one=shift_one, gain_two=gain_two, shift_two=shift_two)


EPSILON = 1e-06
NEGATIVE = -1e+30
HIGHEST = lax.Precision.HIGHEST

@jax.custom_vjp
def low(v):
    return lax.optimization_barrier(v.astype(jnp.bfloat16)).astype(jnp.float32)

@jax.custom_vjp
def low_back(v):
    return v

def low_keep(v):
    return (low(v), None)

def low_pass(kept, grad):
    return (grad,)

def back_keep(v):
    return (v, None)

def back_low(kept, grad):
    return (low(grad),)
low.defvjp(low_keep, low_pass)
low_back.defvjp(back_keep, back_low)

def layer_norm(values_in, gain_vec, shift_vec):
    center = lax.optimization_barrier(jnp.mean(values_in, axis=-1, keepdims=True))
    centered = values_in - center
    spread = lax.optimization_barrier(jnp.mean(centered * centered, axis=-1, keepdims=True))
    return centered * lax.rsqrt(spread + EPSILON) * gain_vec + shift_vec

def clip_forward(clip_rows, params):
    w_qkv, query_bias, value_bias, w_proj, proj_bias, w_up, up_bias, w_down, down_bias, gain_one, shift_one, gain_two, shift_two = params
    head_size = D // HEADS
    normed_one = low(layer_norm(clip_rows, gain_one, shift_one))
    projected = jnp.dot(normed_one, w_qkv, precision=HIGHEST)
    queries = low_back(low(projected[:, :D] + query_bias)).reshape(POS, HEADS, head_size)
    key_rows = low_back(low(projected[:, D:2 * D])).reshape(POS, HEADS, head_size)
    value_rows = low_back(low(projected[:, 2 * D:] + value_bias)).reshape(POS, HEADS, head_size)
    raw = jnp.einsum('qhd,khd->hqk', queries, key_rows, precision=HIGHEST) * head_size ** (-0.5)
    raw = low_back(raw)
    frame_of = jnp.arange(POS, dtype=jnp.int32) // HW
    allowed = jnp.abs(frame_of[:, None] - frame_of[None, :]) <= 1
    scores = jnp.where(allowed[None], raw, NEGATIVE)
    top_score = lax.optimization_barrier(jnp.max(scores, axis=-1, keepdims=True))
    expo = jnp.exp(scores - top_score)
    probs = low(expo / lax.optimization_barrier(jnp.sum(expo, axis=-1, keepdims=True)))
    context = jnp.einsum('hqk,khd->qhd', probs, value_rows, precision=HIGHEST).reshape(POS, D)
    context = low_back(low(context))
    attended = low_back(jnp.dot(context, w_proj, precision=HIGHEST) + proj_bias)
    middle = clip_rows + attended
    normed_two = low(layer_norm(middle, gain_two, shift_two))
    pre_act = low_back(jnp.dot(normed_two, w_up, precision=HIGHEST) + up_bias)
    activated = low(jax.nn.gelu(pre_act, approximate=False))
    return middle + jnp.dot(activated, w_down, precision=HIGHEST) + down_bias

def group_moments(outputs, view_masks, view_group):
    member = (view_group[:, :, None] == jnp.arange(GROUPS, dtype=jnp.int32)[None, None, :]).astype(jnp.float32)
    weight_rows = jnp.einsum('cvg,cvp->cgp', member, view_masks.astype(jnp.float32), precision=HIGHEST)
    counts = lax.optimization_barrier(jnp.sum(weight_rows, axis=-1))
    first_sums = jnp.einsum('cgp,cpd->cgd', weight_rows, outputs, precision=HIGHEST)
    second_sums = jnp.einsum('cgp,cpd->cgd', weight_rows, outputs * outputs, precision=HIGHEST)
    floor_counts = jnp.maximum(counts, 1.0)[:, :, None]
    group_mean = first_sums / floor_counts
    group_var = second_sums / floor_counts - group_mean * group_mean
    return jnp.stack([group_mean, group_var], axis=2)

def reference(tokens, out_grad, view_masks, view_group, w_qkv, query_bias, value_bias, w_proj, proj_bias, w_up, up_bias, w_down, down_bias, gain_one, shift_one, gain_two, shift_two):
    params = tuple((item.astype(jnp.float32) for item in (w_qkv, query_bias, value_bias, w_proj, proj_bias, w_up, up_bias, w_down, down_bias, gain_one, shift_one, gain_two, shift_two)))
    inputs = tokens.astype(jnp.float32)

    def forward(input_rows, param_set):
        outputs = lax.map(jax.checkpoint(lambda clip_rows: clip_forward(clip_rows, param_set)), input_rows)
        return (outputs, group_moments(outputs, view_masks, view_group))
    (outputs, group_stats), pullback = jax.vjp(forward, inputs, params)
    grad_inputs, grad_params = pullback((out_grad.astype(jnp.float32), jnp.zeros_like(group_stats)))
    return (outputs.astype(jnp.bfloat16), group_stats, grad_inputs.astype(jnp.bfloat16), grad_params[0], grad_params[1], grad_params[2], grad_params[3], grad_params[4], grad_params[5], grad_params[6], grad_params[7], grad_params[8], grad_params[9], grad_params[10], grad_params[11], grad_params[12])
```

```python
import functools

import jax
import jax.numpy as jnp
from jax import lax
from jax.experimental import pallas as pl
from jax.experimental.pallas import tpu as pltpu
from jax.sharding import PartitionSpec as P

HEADS = 6
NF = 8
HW = 196
GROUPS = 2
EPSILON = 1e-06
NEGATIVE = -1e30
MESH = pl.DeviceIdType.MESH
f32 = jnp.float32
bf16 = jnp.bfloat16

D = 384
FF = 1536
KR = 208
QL = 256
QB, VB, PB, UB, DB, G1, S1, G2, S2 = 0, 1, 2, 3, 7, 8, 9, 10, 11
ROWS_A = 2 * FF + D
ROWS_B = 3 * D


def dot(a, b):
    return lax.dot_general(a, b, (((1,), (0,)), ((), ())), preferred_element_type=f32)


def dot_t(a, b):
    return lax.dot_general(a, b, (((1,), (1,)), ((), ())), preferred_element_type=f32)


def iota(shape, dim):
    return lax.broadcasted_iota(jnp.int32, shape, dim)


def low(v):
    return v.astype(bf16)


def wide(v):
    return jnp.concatenate([v, v], axis=1)


def fold(v):
    return v[:, 0:128] + v[:, 128:256]


def eye(n):
    return low(jnp.where(iota((n, n), 0) == iota((n, n), 1), 1.0, 0.0))


def ds(start, size, step):
    return pl.ds(pl.multiple_of(start, step), size)


def when(condition, action):
    if condition is None:
        action()
    else:
        pl.when(condition)(action)


def piece_rows(quarter, nz):
    return next(p for p in range(16, quarter + 1, 16) if quarter % p == 0 and p * nz >= quarter)


class Reduce:
    def __init__(self, rows, g, sb, ag, r2, r3, send, recv, me, nf, nz):
        self.rows, self.g, self.sb, self.ag, self.r2, self.r3 = rows, g, sb, ag, r2, r3
        self.send, self.recv, self.nf, self.nz = send, recv, nf, nz
        self.f, clip = me
        self.core, self.z = lax.rem(clip, 2), lax.div(clip, 2)
        self.half = rows // 2
        self.quarter = self.half // nf
        self.piece = piece_rows(self.quarter, nz)
        self.owners = self.quarter // self.piece
        self.base = self.core * self.half
        self.qbase = self.base + self.f * self.quarter
        self.pbase = self.qbase + self.z * self.piece

    def at(self, start, size, ref=None):
        return (self.ag if ref is None else ref).at[ds(start, size, 16), :]

    def copies(self, stage):
        nf, nz, out = self.nf, self.nz, []
        if stage == 1:
            o = self.at((1 - self.core) * self.half, self.half, self.sb)
            out = [(o, o, (self.f, self.z * 2 + 1 - self.core), 0, None, None)]
        if stage in (2, 5):
            for k in range(1, nf):
                t = lax.rem(self.f + k, nf)
                dev = (t, self.z * 2 + self.core)
                if stage == 2:
                    src = self.at(self.base + t * self.quarter, self.quarter, self.sb)
                    out.append((src, self.r2.at[k - 1], dev, k, None, None))
                else:
                    src = self.at(self.qbase, self.quarter)
                    out.append((src, src, dev, nf + 2 * nz + k - 3, None, None))
        if stage in (3, 4):
            mine = None if self.owners == nz else self.z < self.owners
            for k in range(1, nz):
                t = lax.rem(self.z + k, nz)
                s = lax.rem(self.z + nz - k, nz)
                dev = (self.f, t * 2 + self.core)
                theirs = None if self.owners == nz else t < self.owners
                comes = None if self.owners == nz else s < self.owners
                if stage == 3:
                    src = self.at(self.qbase + t * self.piece, self.piece, self.sb)
                    out.append((src, self.r3.at[k - 1], dev, nf + k - 1, theirs, mine))
                else:
                    src = self.at(self.pbase, self.piece)
                    out.append((src, src, dev, nf + nz + k - 2, mine, comes))
        if stage == 6:
            s = self.at(self.base, self.half)
            dev = (self.f, self.z * 2 + 1 - self.core)
            out = [(s, s, dev, 2 * nf + 2 * nz - 3, None, None)]
        return [
            (
                pltpu.make_async_remote_copy(
                    src_ref=s,
                    dst_ref=d,
                    send_sem=self.send.at[i],
                    recv_sem=self.recv.at[i],
                    device_id=dev,
                    device_id_type=MESH,
                ),
                sent,
                comes,
            )
            for s, d, dev, i, sent, comes in out
        ]

    def start(self, stage):
        for c, sent, _ in self.copies(stage):
            when(sent, c.start)

    def wait(self, stage):
        for c, sent, comes in self.copies(stage):
            when(comes, c.wait_recv)
            when(sent, c.wait_send)

    def step(self, stage):
        if stage > 1:
            self.wait(stage - 1)
        g, sb, ag = self.g, self.sb, self.ag
        if stage == 1:
            rows = ds((1 - self.core) * self.half, self.half, 16)
            sb[rows, :] = low(g[rows, :])
        if stage == 2:
            rows = ds(self.base, self.half, 16)
            total = g[rows, :] + sb[rows, :].astype(f32)
            g[rows, :] = total
            sb[rows, :] = low(total)
        if stage == 3:
            rows = ds(self.qbase, self.quarter, 16)
            total = g[rows, :]
            for k in range(self.nf - 1):
                total += self.r2[k].astype(f32)
            g[rows, :] = total
            sb[rows, :] = low(total)
        if stage == 4:

            def sum_piece():
                rows = ds(self.pbase, self.piece, 16)
                total = g[rows, :]
                for k in range(self.nz - 1):
                    total += self.r3[k].astype(f32)
                ag[rows, :] = low(total)

            when(None if self.owners == self.nz else self.z < self.owners, sum_piece)
        if stage < 7:
            self.start(stage)

    @staticmethod
    def count(nf, nz):
        return 2 * nf + 2 * nz - 2


def body(
    nf,
    nz,
    rows_a,
    rows_b,
    tok,
    og,
    masks,
    grp,
    wqkv,
    wp,
    wu,
    wd,
    vecs,
    bout,
    stats,
    gtok,
    out_a,
    out_b,
    wqkvT,
    wpT,
    wuT,
    wdT,
    cb,
    TI,
    OS,
    xs,
    ys,
    mw,
    XT,
    n1T,
    NR,
    QT,
    KT,
    VT,
    Kr,
    Vr,
    ctxT,
    n2T,
    actT,
    dpreT,
    gattT,
    dyR,
    dOT,
    ST,
    dmid,
    DQ,
    DK,
    DV,
    acc,
    SP,
    SPr,
    GA,
    GB,
    SB,
    agA,
    agB,
    r2A,
    r3A,
    r2B,
    r3B,
    nr_send,
    nr_recv,
    do_send,
    do_recv,
    st_send,
    st_recv,
    sp_send,
    sp_recv,
    sendA,
    recvA,
    sendB,
    recvB,
    out_sem,
    in_sem,
    row_sem,
):
    clips = tok.shape[0]
    rows = tok.shape[1]
    me_f = lax.axis_index("frame")
    me_c = lax.axis_index("clip")
    core, zi = lax.rem(me_c, 2), lax.div(me_c, 2)
    first, last = me_f == 0, me_f == nf - 1

    def fetch(ref, k, c):
        return pltpu.make_async_copy(ref.at[c], TI.at[c], in_sem.at[k, c])

    def put(n, ref, c):
        slot = lax.rem(n, 2)
        cp = pltpu.make_async_copy(OS.at[slot], ref.at[c], row_sem.at[slot])
        pl.when(n >= 2)(cp.wait)
        OS[slot] = low(ys[0:rows, :])
        cp.start()

    for c in range(clips):
        fetch(tok, 0, c).start()

    NR[...] = jnp.zeros(NR.shape, bf16)
    for c in range(clips):
        for s in (0, 3):
            dOT[c * 4 + s] = jnp.zeros(dOT.shape[1:], bf16)
            ST[c * 4 + s] = jnp.where(iota((3, 8, QL), 1) < 2, 1e30, 0.0)

    barrier = pltpu.get_barrier_semaphore()
    peers = [(lax.rem(me_f + k, nf), me_c) for k in range(1, nf)]
    peers.append((me_f, zi * 2 + 1 - core))
    peers += [(me_f, lax.rem(zi + k, nz) * 2 + core) for k in range(1, nz)]
    for peer in peers:
        pl.semaphore_signal(barrier, inc=1, device_id=peer, device_id_type=MESH)

    def halo(src, dst, send, recv, to_right):
        return pltpu.make_async_remote_copy(
            src_ref=src,
            dst_ref=dst,
            send_sem=send,
            recv_sem=recv,
            device_id=((me_f + 1) if to_right else (me_f - 1), me_c),
            device_id_type=MESH,
        )

    def nr_copy(c, right):
        i, o, k = (2, 0, 0) if right else (1, 3, 1)
        return halo(
            NR.at[c * 4 + i, pl.ds(0, KR)],
            NR.at[c * 4 + o, pl.ds(0, KR)],
            nr_send.at[c, k],
            nr_recv.at[c, k],
            right,
        )

    def do_copies(c, right):
        i, o, k = (2, 0, 0) if right else (1, 3, 1)
        return (
            halo(
                dOT.at[c * 4 + i], dOT.at[c * 4 + o], do_send.at[c, k], do_recv.at[c, k], right
            ),
            halo(ST.at[c * 4 + i], ST.at[c * 4 + o], st_send.at[c, k], st_recv.at[c, k], right),
        )

    def each_side(start, make):
        for right, here, there in ((True, last, first), (False, first, last)):

            @pl.when(jnp.logical_not(here))
            def _():
                for cp in make(right):
                    if start:
                        cp.start()
                    else:
                        cp.wait_send()

            if not start:

                @pl.when(jnp.logical_not(there))
                def _():
                    for cp in make(right):
                        cp.wait_recv()

    xs[...] = jnp.zeros(xs.shape, f32)
    mw[...] = jnp.zeros(mw.shape, f32)
    one_d = eye(D)
    one_q = eye(QL)

    def column(i):
        return wide(cb[i])

    for i in range(12):
        cb[i] = jnp.transpose(jnp.broadcast_to(vecs[i : i + 1, :], (128, D)))
    n1T[...] = jnp.ones(n1T.shape, bf16)
    n2T[...] = jnp.ones(n2T.shape, bf16)
    ctxT[...] = jnp.ones(ctxT.shape, bf16)
    pl.semaphore_wait(barrier, len(peers))

    def frame_rows(f):
        v = xs[pl.ds(HW * f, KR), :]
        tail = jnp.where(iota((16, D), 0) < HW - (KR - 16), v[KR - 16 :], 0.0)
        return low(jnp.concatenate([v[: KR - 16], tail, jnp.zeros((QL - KR, D), f32)], axis=0))

    def norm_one(c, _):
        fetch(tok, 0, c).wait()
        xs[0:rows, :] = TI[c].astype(f32)
        fetch(og, 1, c).start()
        for f in range(2):
            xT = dot_t(one_d, frame_rows(f))
            XT[c * 2 + f] = low(xT)
            cent = xT - jnp.sum(xT, axis=0, keepdims=True) * (1.0 / D)
            var = jnp.sum(cent * cent, axis=0, keepdims=True) * (1.0 / D)
            nT = low(cent * lax.rsqrt(var + EPSILON) * column(G1) + column(S1))
            n1T[c, 0:D, f * QL : (f + 1) * QL] = nT
            NR[c * 4 + f + 1, 0:KR, :] = low(dot_t(one_q[0:KR], nT))
        each_side(True, lambda right: (nr_copy(c, right),))
        return 0

    lax.fori_loop(0, clips, norm_one, 0)

    for j in range(3):
        wqkvT[j * D : (j + 1) * D, :] = low(dot_t(one_d, wqkv[:, j * D : (j + 1) * D]))
    wpT[...] = low(dot_t(one_d, wp[...]))
    for j in range(4):
        wuT[j * D : (j + 1) * D, :] = low(dot_t(one_d, wu[:, j * D : (j + 1) * D]))
        wdT[:, j * D : (j + 1) * D] = low(dot_t(one_d, wd[j * D : (j + 1) * D, :]))
    for r in (GA, GB, acc):
        r[...] = jnp.zeros(r.shape, f32)
    DK[...] = jnp.zeros(DK.shape, bf16)
    KT[...] = jnp.zeros(KT.shape, bf16)
    DV[...] = jnp.zeros(DV.shape, bf16)

    before_bias = jnp.where(first, NEGATIVE, 0.0).astype(f32)
    after_bias = jnp.where(last, NEGATIVE, 0.0).astype(f32)
    z64 = jnp.zeros((64, QL), bf16)
    zpad = jnp.zeros((QL - KR, QL), bf16)

    def split_heads(v):
        return (
            jnp.concatenate([v[0:64], z64], axis=0),
            jnp.concatenate([z64, v[64:128]], axis=0),
        )

    def project(c, s):
        i = c * 4 + s
        qT = low(low(dot_t(wqkvT[0:D, :], NR[i]) + column(QB)) * 0.125)
        vT = low(dot_t(wqkvT[2 * D :, :], NR[i]) + column(VB))
        k = low(dot(NR[i, 0:KR], wqkv[:, D : 2 * D]))
        v = low(dot(NR[i, 0:KR], wqkv[:, 2 * D :]) + vecs[VB : VB + 1, :])
        for p in range(3):
            sl = slice(p * 128, (p + 1) * 128)
            QT[i, p] = qT[sl]
            VT[s, p] = vT[sl]
            Kr[i, p] = k[:, sl]
            Vr[i, p] = v[:, sl]

    def forward_pair(c, p):
        for f in range(2):
            i = c * 4 + f + 1
            out = []
            for hh, qm in enumerate(split_heads(QT[i, p])):
                parts = []
                for j in range(3):
                    s = dot(Kr[c * 4 + f + j, p], qm)
                    tail = jnp.where(iota((16, QL), 0) < HW - (KR - 16), s[KR - 16 :], NEGATIVE)
                    s = jnp.concatenate([s[: KR - 16], tail], axis=0)
                    if f + j == 0:
                        s = s + before_bias
                    if f + j == 3:
                        s = s + after_bias
                    parts.append(s)
                top = functools.reduce(
                    jnp.maximum, [jnp.max(s, axis=0, keepdims=True) for s in parts]
                )
                total = jnp.zeros((1, QL), f32)
                ctx = jnp.zeros((64, QL), f32)
                for j in range(3):
                    e = jnp.exp(parts[j] - top)
                    total += jnp.sum(e, axis=0, keepdims=True)
                    e = jnp.concatenate([low(e), zpad], axis=0)
                    ctx += dot(VT[f + j, p, hh * 64 : hh * 64 + 64, :], e)
                out.append(ctx / total)
                ST[i, p, hh : hh + 1, :] = top + jnp.log(total)
            ctxT[ds(p * 128, 128, 128), f * QL : (f + 1) * QL] = low(
                jnp.concatenate(out, axis=0)
            )

    def gelu_parts(v):
        z = jnp.abs(v) * 0.7071067811865476
        t = 1.0 / (1.0 + 0.3275911 * z)
        e = jnp.exp(v * v * -0.5)
        poly = 0.5 * 1.061405429
        poly = poly * t + 0.5 * -1.453152027
        poly = poly * t + 0.5 * 1.421413741
        poly = poly * t + 0.5 * -0.284496736
        poly = poly * t + 0.5 * 0.254829592
        h = poly * t * e
        phi = jnp.where(v >= 0, 1.0 - h, h)
        return phi, v * (e * 0.3989422804014327)

    def feed_forward(c, f):
        b = c * 2 + f
        lanes = slice(f * QL, (f + 1) * QL)
        xT = XT[b].astype(f32)
        mid = xT + (dot(wpT[...], ctxT[0:D, lanes]) + column(PB))
        cent = mid - jnp.sum(mid, axis=0, keepdims=True) * (1.0 / D)
        var = jnp.sum(cent * cent, axis=0, keepdims=True) * (1.0 / D)
        r = lax.rsqrt(var + EPSILON)
        xh = cent * r
        nT = low(xh * column(G2) + column(S2))
        n2T[0:D, lanes] = nT
        dy = frame_rows(f)
        dyR[lanes, :] = dy
        dyT = dot_t(one_d, dy)
        dyl = low(dyT)
        outT = mid + column(DB)
        dn = jnp.zeros((D, QL), f32)
        for j in range(4):
            sl = slice(j * D, (j + 1) * D)
            pre = dot(wuT[sl, :], nT) + column(UB + j)
            phi, slope = gelu_parts(pre)
            act = low(pre * phi)
            actT[sl, lanes] = act
            dpre = low(dot(wd[sl, :], dyl) * (phi + slope))
            dpreT[sl, lanes] = dpre
            outT += dot(wdT[:, sl], act)
            dn += dot(wu[:, sl], dpre)
        outl = low(outT)
        ys[pl.ds(HW * f, KR), :] = dot_t(one_q[0:KR], outl)
        sq = outT * outT
        out2 = low(outT - outl.astype(f32))
        sql = low(sq)
        sq2 = low(sq - sql.astype(f32))
        m = mw[...]
        if f == 1:
            m = pltpu.roll(m, 2 * QL - HW, 1)
        m = jnp.where(iota((8, QL), 1) < HW, m[:, 0:QL], 0.0)
        w = []
        for g in range(GROUPS):
            w.append(
                sum(
                    m[v : v + 1, :] * jnp.where(grp[c, v] == g, 1.0, 0.0).astype(f32)
                    for v in range(2)
                )
            )
        row = iota((16, QL), 0)

        def place(k):
            return jnp.where(row == k, w[0], jnp.where(row == k + 1, w[1], 0.0))

        w1, w2 = low(place(0)), low(place(2))
        cnt = jnp.sum(place(4), axis=1, keepdims=True)
        sums = dot_t(w1, outl) + dot_t(w1, out2) + dot_t(w2, sql) + dot_t(w2, sq2) + cnt
        if f == 0:
            SP[c] = sums[0:8]
        else:
            SP[c] = SP[c] + sums[0:8]
        acc[0] += fold(dn * xh)
        acc[1] += fold(dn)
        gg = dn * column(G2)
        m1 = jnp.sum(gg, axis=0, keepdims=True) * (1.0 / D)
        m2 = jnp.sum(gg * xh, axis=0, keepdims=True) * (1.0 / D)
        gm = dyT + r * (gg - m1 - xh * m2)
        dmid[b] = gm
        ga = low(gm)
        gattT[:, lanes] = ga
        gc = low(dot(wp[...], ga))
        i = c * 4 + f + 1
        prod = gc.astype(f32) * ctxT[0:D, lanes].astype(f32)
        for h in range(HEADS):
            ST[i, h // 2, 2 + h % 2 : 3 + h % 2, :] = jnp.sum(
                prod[h * 64 : h * 64 + 64], axis=0, keepdims=True
            )
        for p in range(3):
            dOT[i, p] = gc[p * 128 : (p + 1) * 128]

    def weight_grads():
        def chunk(j, _):
            at = ds(j * D, D, D)
            GA[at, :] += dot(actT[at, :], dyR[...])
            g = dot_t(n2T[...], dpreT[at, :])
            GA[ds(FF + j * D, D, D), :] += g[0:D]
            GA[pl.ds(ROWS_A + j, 1), :] += g[D : D + 1]
            return 0

        lax.fori_loop(0, 4, chunk, 0)
        g = dot_t(ctxT[...], gattT[...])
        GA[2 * FF : 2 * FF + D, :] += g[0:D]
        GA[ROWS_A + 4 : ROWS_A + 5, :] += g[D : D + 1]
        GA[ROWS_A + 5 : ROWS_A + 6, :] += dot(n2T[D : D + 16, :], dyR[...])[0:1]

    def front(c, _):
        project(c, 1)
        project(c, 2)
        each_side(False, lambda right: (nr_copy(c, right),))
        project(c, 0)
        project(c, 3)

        def pair(p, _):
            forward_pair(c, p)
            return 0

        lax.fori_loop(0, 3, pair, 0)
        fetch(og, 1, c).wait()
        xs[0:rows, :] = TI[c].astype(f32)
        mw[0:2, 0:rows] = masks[c].astype(f32)
        for f in range(2):
            feed_forward(c, f)
        each_side(True, lambda right: do_copies(c, right))
        put(c, bout, c)
        weight_grads()
        return 0

    lax.fori_loop(0, clips, front, 0)

    def gather_rows(ref, row, k):
        ref[row : row + 1, :] = jnp.sum(jnp.transpose(acc[k]), axis=0, keepdims=True)

    gather_rows(GA, ROWS_A + 6, 0)
    gather_rows(GA, ROWS_A + 7, 1)

    me = (me_f, me_c)
    redA = Reduce(rows_a, GA, SB, agA, r2A, r3A, sendA, recvA, me, nf, nz)
    redB = Reduce(rows_b, GB, SB, agB, r2B, r3B, sendB, recvB, me, nf, nz)

    def sp_copies():
        return [
            pltpu.make_async_remote_copy(
                src_ref=SP,
                dst_ref=SPr.at[k - 1],
                send_sem=sp_send.at[k - 1],
                recv_sem=sp_recv.at[k - 1],
                device_id=(lax.rem(me_f + k, nf), me_c),
                device_id_type=MESH,
            )
            for k in range(1, nf)
        ]

    for cp in sp_copies():
        cp.start()

    def back_block(i, g, p, qms, doms, own):
        out_q, gk, gv = [], jnp.zeros((KR, 128), f32), jnp.zeros((KR, 128), f32)
        for hh in range(2):
            lse = ST[i, p, hh : hh + 1, :]
            delta = ST[i, p, 2 + hh : 3 + hh, :]
            s = dot(Kr[g, p], qms[hh])
            pr = jnp.exp(s - lse)
            if own[2] is not None:
                pr = pr * own[2]
            tail = jnp.where(iota((16, QL), 0) < HW - (KR - 16), pr[KR - 16 :], 0.0)
            pr = jnp.concatenate([pr[: KR - 16], tail], axis=0)
            dp = dot(Vr[g, p], doms[hh])
            dsc = low(pr * (dp - delta))
            if own[1]:
                gv += dot_t(low(pr), doms[hh])
                gk += dot_t(dsc, qms[hh])
            if own[0]:
                dsp = jnp.concatenate([dsc, zpad], axis=0)
                out_q.append(dot(KT[lax.rem(g, 4), p, hh * 64 : hh * 64 + 64, :], dsp))
        return out_q, gk, gv

    has_before = jnp.where(first, 0.0, 1.0).astype(f32)
    has_after = jnp.where(last, 0.0, 1.0).astype(f32)

    def back_pair(c, p):
        gks = [jnp.zeros((KR, 128), f32)] * 2
        gvs = [jnp.zeros((KR, 128), f32)] * 2
        for q in (1, 2, 0, 3):
            i = c * 4 + q
            qms = split_heads(QT[i, p])
            doms = split_heads(dOT[i, p])
            keys = {1: (0, 1, 2), 2: (1, 2, 3), 0: (1,), 3: (2,)}[q]
            total = [jnp.zeros((64, QL), f32)] * 2
            for g in keys:
                keep = {0: has_before, 3: has_after}.get(g)
                own = (q in (1, 2), g in (1, 2), keep)
                dq, gk, gv = back_block(i, c * 4 + g, p, qms, doms, own)
                if own[0]:
                    total = [total[0] + dq[0], total[1] + dq[1]]
                if own[1]:
                    gks[g - 1] = gks[g - 1] + gk
                    gvs[g - 1] = gvs[g - 1] + gv
            if q in (1, 2):
                DQ[q - 1, ds(p * 128, 128, 128), :] = low(
                    jnp.concatenate(total, axis=0) * 0.125
                )
        for f in range(2):
            DK[f, p, 0:KR, :] = low(gks[f])
            DV[f, p, 0:KR, :] = low(gvs[f])

    redA.step(1)

    def back(c, _):
        each_side(False, lambda right: do_copies(c, right))
        for g in range(4):
            for p in range(3):
                KT[g, p, :, 0:KR] = low(dot_t(one_q[0:128, 0:128], Kr[c * 4 + g, p]))

        def pair(p, _):
            back_pair(c, p)
            it = c * 3 + p
            for stage, when in ((2, 1), (3, 4), (4, 6), (5, 8), (6, 10)):

                @pl.when(it == when)
                def _():
                    redA.step(stage)

            return 0

        lax.fori_loop(0, 3, pair, 0)
        dqs, dks, dvs = [], [], []
        for f in range(2):
            b = c * 2 + f
            dq = DQ[f]
            dk = jnp.concatenate([DK[f, p] for p in range(3)], axis=1)
            dv = jnp.concatenate([DV[f, p] for p in range(3)], axis=1)
            dqs.append(dq)
            dks.append(dk)
            dvs.append(dv)
            dn = dot(wqkv[:, 0:D], dq) + dot_t(wqkv[:, D : 2 * D], dk)
            dn += dot_t(wqkv[:, 2 * D :], dv)
            xT = XT[b].astype(f32)
            cent = xT - jnp.sum(xT, axis=0, keepdims=True) * (1.0 / D)
            var = jnp.sum(cent * cent, axis=0, keepdims=True) * (1.0 / D)
            r = lax.rsqrt(var + EPSILON)
            xh = cent * r
            acc[2] += fold(dn * xh)
            acc[3] += fold(dn)
            gg = dn * column(G1)
            m1 = jnp.sum(gg, axis=0, keepdims=True) * (1.0 / D)
            m2 = jnp.sum(gg * xh, axis=0, keepdims=True) * (1.0 / D)
            gT = low(dmid[b] + r * (gg - m1 - xh * m2))
            ys[pl.ds(HW * f, KR), :] = dot_t(one_q[0:KR], gT)
        put(clips + c, gtok, c)
        n1 = n1T[c]
        g = dot_t(n1, jnp.concatenate(dqs, axis=1))
        GB[0:D, :] += g[0:D]
        GB[ROWS_B : ROWS_B + 1, :] += g[D : D + 1]
        GB[D : 2 * D, :] += dot(n1[0:D], jnp.concatenate(dks, axis=0))
        g = dot(n1, jnp.concatenate(dvs, axis=0))
        GB[2 * D : 3 * D, :] += g[0:D]
        GB[ROWS_B + 1 : ROWS_B + 2, :] += g[D : D + 1]
        return 0

    lax.fori_loop(0, clips, back, 0)
    gather_rows(GB, ROWS_B + 2, 2)
    gather_rows(GB, ROWS_B + 3, 3)

    redA.step(7)
    redB.step(1)
    copy_a = pltpu.make_async_copy(agA, out_a, out_sem.at[0])
    copy_a.start()
    for cp in sp_copies():
        cp.wait()
    for c in range(clips):
        t = SP[c] + sum(SPr[k, c] for k in range(nf - 1))
        inv = 1.0 / jnp.maximum(t[4:6], 1.0)
        mean = t[0:2] * inv
        var = t[2:4] * inv - mean * mean
        stats[c, 0:1, :] = mean[0:1]
        stats[c, 1:2, :] = var[0:1]
        stats[c, 2:3, :] = mean[1:2]
        stats[c, 3:4, :] = var[1:2]
    for stage in range(2, 8):
        redB.step(stage)
    copy_b = pltpu.make_async_copy(agB, out_b, out_sem.at[1])
    copy_b.start()
    for slot in range(2):
        pltpu.make_async_copy(OS.at[slot], gtok.at[0], row_sem.at[slot]).wait()
    copy_a.wait()
    copy_b.wait()


def local(nf, nz, tokens, out_grad, view_masks, view_group, *params):
    w_qkv, query_bias, value_bias, w_proj, proj_bias, w_up, up_bias, w_down = params[:8]
    down_bias, gain_one, shift_one, gain_two, shift_two = params[8:]
    clips, rows, width = tokens.shape
    unit = 512
    rows_a = -(-(ROWS_A + 8) // unit) * unit
    rows_b = -(-(ROWS_B + 4) // unit) * unit
    vecs = jnp.concatenate(
        [
            query_bias,
            value_bias,
            proj_bias,
            up_bias,
            down_bias,
            gain_one,
            shift_one,
            gain_two,
            shift_two,
        ]
    ).reshape(12, D)
    vmem = pl.BlockSpec(memory_space=pltpu.VMEM)
    hbm = pl.BlockSpec(memory_space=pl.ANY)
    sems = pltpu.SemaphoreType.DMA
    n_red = Reduce.count(nf, nz)
    bout, stats, gtok, out_a, out_b = pl.pallas_call(
        functools.partial(body, nf, nz, rows_a, rows_b),
        out_shape=(
            jax.ShapeDtypeStruct((clips, rows, D), bf16),
            jax.ShapeDtypeStruct((clips, 4, D), f32),
            jax.ShapeDtypeStruct((clips, rows, D), bf16),
            jax.ShapeDtypeStruct((rows_a, D), bf16),
            jax.ShapeDtypeStruct((rows_b, D), bf16),
        ),
        in_specs=[hbm, hbm, vmem, pl.BlockSpec(memory_space=pltpu.SMEM)] + [vmem] * 5,
        out_specs=(hbm, vmem, hbm, hbm, hbm),
        scratch_shapes=[
            pltpu.VMEM((3 * D, D), bf16),
            pltpu.VMEM((D, D), bf16),
            pltpu.VMEM((FF, D), bf16),
            pltpu.VMEM((D, FF), bf16),
            pltpu.VMEM((12, D, 128), f32),
            pltpu.VMEM((clips, rows, D), bf16),
            pltpu.VMEM((2, rows, D), bf16),
            pltpu.VMEM((416, D), f32),
            pltpu.VMEM((416, D), f32),
            pltpu.VMEM((8, 2 * QL), f32),
            pltpu.VMEM((clips * 2, D, QL), bf16),
            pltpu.VMEM((clips, D + 16, 2 * QL), bf16),
            pltpu.VMEM((clips * 4, QL, D), bf16),
            pltpu.VMEM((clips * 4, 3, 128, QL), bf16),
            pltpu.VMEM((4, 3, 128, QL), bf16),
            pltpu.VMEM((4, 3, 128, QL), bf16),
            pltpu.VMEM((clips * 4, 3, KR, 128), bf16),
            pltpu.VMEM((clips * 4, 3, KR, 128), bf16),
            pltpu.VMEM((D + 16, 2 * QL), bf16),
            pltpu.VMEM((D + 16, 2 * QL), bf16),
            pltpu.VMEM((FF, 2 * QL), bf16),
            pltpu.VMEM((FF, 2 * QL), bf16),
            pltpu.VMEM((D, 2 * QL), bf16),
            pltpu.VMEM((2 * QL, D), bf16),
            pltpu.VMEM((clips * 4, 3, 128, QL), bf16),
            pltpu.VMEM((clips * 4, 3, 8, QL), f32),
            pltpu.VMEM((clips * 2, D, QL), f32),
            pltpu.VMEM((2, D, QL), bf16),
            pltpu.VMEM((2, 3, QL, 128), bf16),
            pltpu.VMEM((2, 3, QL, 128), bf16),
            pltpu.VMEM((4, D, 128), f32),
            pltpu.VMEM((clips, 8, D), f32),
            pltpu.VMEM((nf - 1, clips, 8, D), f32),
            pltpu.VMEM((rows_a, D), f32),
            pltpu.VMEM((rows_b, D), f32),
            pltpu.VMEM((max(rows_a, rows_b), D), bf16),
            pltpu.VMEM((rows_a, D), bf16),
            pltpu.VMEM((rows_b, D), bf16),
            pltpu.VMEM((nf - 1, rows_a // (2 * nf), D), bf16),
            pltpu.VMEM((nz - 1, piece_rows(rows_a // (2 * nf), nz), D), bf16),
            pltpu.VMEM((nf - 1, rows_b // (2 * nf), D), bf16),
            pltpu.VMEM((nz - 1, piece_rows(rows_b // (2 * nf), nz), D), bf16),
            sems((clips, 2)),
            sems((clips, 2)),
            sems((clips, 2)),
            sems((clips, 2)),
            sems((clips, 2)),
            sems((clips, 2)),
            sems((nf - 1,)),
            sems((nf - 1,)),
            sems((n_red,)),
            sems((n_red,)),
            sems((n_red,)),
            sems((n_red,)),
            sems((2,)),
            sems((2, clips)),
            sems((2,)),
        ],
        compiler_params=pltpu.CompilerParams(
            collective_id=0, has_side_effects=True, vmem_limit_bytes=64 * 1024 * 1024 - 65536
        ),
    )(tokens, out_grad, view_masks, view_group, w_qkv, w_proj, w_up, w_down, vecs)

    def side(block, n):
        return block.reshape(n, D, D).transpose(1, 0, 2).reshape(D, n * D).astype(f32)

    def vec(a, row, n=1):
        return a[row : row + n].reshape(n * D).astype(f32)

    return (
        bout,
        stats.reshape(clips, GROUPS, 2, D),
        gtok,
        side(out_b[0 : 3 * D], 3),
        vec(out_b, ROWS_B),
        vec(out_b, ROWS_B + 1),
        out_a[2 * FF : 2 * FF + D].astype(f32),
        vec(out_a, ROWS_A + 4),
        side(out_a[FF : 2 * FF], 4),
        vec(out_a, ROWS_A, 4),
        out_a[0:FF].astype(f32),
        vec(out_a, ROWS_A + 5),
        vec(out_b, ROWS_B + 2),
        vec(out_b, ROWS_B + 3),
        vec(out_a, ROWS_A + 6),
        vec(out_a, ROWS_A + 7),
    )


def solution(mesh):
    row = P("clip", "frame", None)
    in_specs = (row, row, P("clip", None, "frame"), P("clip", None)) + (P(),) * 13
    out_specs = (row, P("clip", None, None, None), row) + (P(),) * 13
    step = functools.partial(local, mesh.shape["frame"], mesh.shape["clip"] // 2)
    return jax.shard_map(step, mesh=mesh, in_specs=in_specs, out_specs=out_specs, check_vma=False)
```

```python
import functools

import jax
import jax.numpy as jnp
from jax import lax
from jax.experimental import pallas as pl
from jax.experimental.pallas import tpu as pltpu
from jax.sharding import PartitionSpec as P

HEADS = 6
NF = 8
HW = 196
GROUPS = 2
EPSILON = 1e-06
NEGATIVE = -1e30
MESH = pl.DeviceIdType.MESH
f32 = jnp.float32
bf16 = jnp.bfloat16

D = 384
FF = 1536
KR = 208
QL = 256
QB, VB, PB, UB, DB, G1, S1, G2, S2 = 0, 1, 2, 3, 7, 8, 9, 10, 11
G_UP, G_PROJ, G_QKV = FF, 2 * FF, 2 * FF + D
G_ROWS = G_QKV + 3 * D
CHUNKS = ((0, FF, False), (G_UP, FF, False), (G_PROJ, D, True))
CHUNKS += tuple((G_QKV + k * D, D, True) for k in range(3))
V_UB, V_PB, V_DB, V_G2, V_S2, V_QB, V_VB, V_G1, V_S1 = 0, 4, 5, 6, 7, 8, 9, 10, 11


def dot(a, b):
    return lax.dot_general(a, b, (((1,), (0,)), ((), ())), preferred_element_type=f32)


def dot_t(a, b):
    return lax.dot_general(a, b, (((1,), (1,)), ((), ())), preferred_element_type=f32)


def iota(shape, dim):
    return lax.broadcasted_iota(jnp.int32, shape, dim)


def low(v):
    return v.astype(bf16)


def wide(v):
    return jnp.concatenate([v, v], axis=1)


def fold(v):
    return v[:, 0:128] + v[:, 128:256]


def eye(n):
    return low(jnp.where(iota((n, n), 0) == iota((n, n), 1), 1.0, 0.0))


def ds(start, size, step):
    return pl.ds(pl.multiple_of(start, step), size)


def both(a, b):
    return b if a is None else a if b is None else jnp.logical_and(a, b)


def when(condition, action):
    if condition is None:
        action()
    else:
        pl.when(condition)(action)


def share(rows, n):
    return next(p for p in range(16, rows + 1, 16) if rows % p == 0 and p * n >= rows)


def spans(nf, nz):
    out, start = [], 0
    for _, rows, z_first in CHUNKS:
        n2, n3 = (nz, nf) if z_first else (nf, nz)
        part = share(rows // 2, n2)
        piece = part if z_first else share(part, n3)
        out.append((start, part, start + (n2 - 1) * part, piece))
        start += (n2 - 1) * part + (n3 - 1) * piece
    return out, start


def together(steps):
    steps = list(steps)
    while steps:
        steps = [s for s in steps if next(s, steps) is not steps]


class Reduce:
    def __init__(self, chunk, refs, sems, me, nf, nz):
        self.off, rows, self.z_first = CHUNKS[chunk]
        self.g, self.sb, self.ag, self.land = refs
        self.send, self.recv = sems[0].at[chunk], sems[1].at[chunk]
        self.f, clip = me
        self.core, self.z = lax.rem(clip, 2), lax.div(clip, 2)
        self.half = rows // 2
        self.land2, self.part, self.land3, self.piece = spans(nf, nz)[0][chunk]
        self.size = (nz, nf) if self.z_first else (nf, nz)
        n3 = self.size[1]
        self.own = (self.half // self.part, n3 if self.z_first else self.part // self.piece)
        self.pos = (self.z, self.f) if self.z_first else (self.f, self.z)
        self.base = self.off + self.core * self.half
        self.qbase = self.base + self.pos[0] * self.part
        self.pbase = self.qbase if self.z_first else self.qbase + self.pos[1] * self.piece

    def at(self, start, size, ref=None):
        return (self.ag if ref is None else ref).at[ds(start, size, 16), :]

    def landing(self, level, k):
        start, rows = ((self.land2, self.part), (self.land3, self.piece))[level]
        return self.land.at[pl.ds(start + k * rows, rows), :]

    def owns(self, level, pos=None):
        if self.own[level] == self.size[level]:
            return None
        return (self.pos[level] if pos is None else pos) < self.own[level]

    def peer(self, level, k):
        t = lax.rem(self.pos[level] + k, self.size[level])
        along_z = self.z_first == (level == 0)
        dev = (self.f, t * 2 + self.core) if along_z else (t, self.z * 2 + self.core)
        return t, dev

    def copies(self, stage):
        n2, n3 = self.size
        out = []
        if stage == 1:
            o = self.at(self.off + (1 - self.core) * self.half, self.half, self.sb)
            out = [(o, o, (self.f, self.z * 2 + 1 - self.core), 0, None, None)]
        if stage in (2, 5):
            for k in range(1, n2):
                t, dev = self.peer(0, k)
                if stage == 2:
                    src = self.at(self.base + t * self.part, self.part, self.sb)
                    dst = self.landing(0, k - 1)
                    out.append((src, dst, dev, k, self.owns(0, t), self.owns(0)))
                else:
                    s, _ = self.peer(0, n2 - k)
                    src = self.at(self.qbase, self.part)
                    sem = n2 + 2 * n3 + k - 3
                    out.append((src, src, dev, sem, self.owns(0), self.owns(0, s)))
        if stage == 3 or (stage == 4 and not self.z_first):
            for k in range(1, n3):
                t, dev = self.peer(1, k)
                if stage == 3:
                    first = self.qbase if self.z_first else self.qbase + t * self.piece
                    src = self.at(first, self.piece, self.sb)
                    sent, comes = self.owns(1, t), self.owns(1)
                    out.append((src, self.landing(1, k - 1), dev, n2 + k - 1, sent, comes))
                else:
                    s, _ = self.peer(1, n3 - k)
                    src = self.at(self.pbase, self.piece)
                    out.append((src, src, dev, n2 + n3 + k - 2, self.owns(1), self.owns(1, s)))
            part = self.owns(0)
            if part is not None:
                out = [(*c[:4], both(part, c[4]), both(part, c[5])) for c in out]
        if stage == 6:
            s = self.at(self.base, self.half)
            dev = (self.f, self.z * 2 + 1 - self.core)
            out = [(s, s, dev, 2 * n2 + 2 * n3 - 3, None, None)]
        return [
            (
                pltpu.make_async_remote_copy(
                    src_ref=s,
                    dst_ref=d,
                    send_sem=self.send.at[i],
                    recv_sem=self.recv.at[i],
                    device_id=dev,
                    device_id_type=MESH,
                ),
                sent,
                comes,
            )
            for s, d, dev, i, sent, comes in out
        ]

    def start(self, stage):
        for c, sent, _ in self.copies(stage):
            when(sent, c.start)

    def wait(self, stage):
        for c, sent, comes in self.copies(stage):
            when(comes, c.wait_recv)
            when(sent, c.wait_send)

    def step(self, stage):
        if stage > 1:
            self.wait(stage - 1)
        g, sb, ag = self.g, self.sb, self.ag
        n2, n3 = self.size
        if stage == 1:
            rows = ds(self.off + (1 - self.core) * self.half, self.half, 16)
            sb[rows, :] = low(g[rows, :])
        if stage == 2:
            rows = ds(self.base, self.half, 16)
            total = g[rows, :] + sb[rows, :].astype(f32)
            g[rows, :] = total
            sb[rows, :] = low(total)
        if stage == 3:

            def sum_part():
                rows = ds(self.qbase, self.part, 16)
                total = g[rows, :]
                for k in range(n2 - 1):
                    total += self.landing(0, k)[...].astype(f32)
                g[rows, :] = total
                sb[rows, :] = low(total)

            when(self.owns(0), sum_part)
        if stage == 4:

            def sum_piece():
                rows = ds(self.pbase, self.piece, 16)
                total = g[rows, :]
                for k in range(n3 - 1):
                    total += self.landing(1, k)[...].astype(f32)
                ag[rows, :] = low(total)

            when(both(self.owns(0), self.owns(1)), sum_piece)
        if stage < 7:
            self.start(stage)

    @staticmethod
    def count(nf, nz):
        return 2 * nf + 2 * nz - 2


def body(
    nf,
    nz,
    tok,
    og,
    masks,
    grp,
    wqkv,
    wp,
    wu,
    wd,
    vqb,
    vvb,
    vpb,
    vub,
    vdb,
    vg1,
    vs1,
    vg2,
    vs2,
    bout,
    stats,
    gtok,
    out_g,
    out_v,
    wqvT,
    wpT,
    wuT,
    wdT,
    cb,
    TI,
    OS,
    xs,
    ys,
    mw,
    XT,
    n1T,
    NR,
    QT,
    KT,
    VT,
    Kr,
    Vr,
    ctxT,
    n2T,
    AD,
    gattT,
    dyR,
    dOT,
    dyT,
    FX,
    FY,
    SS,
    PG,
    SG,
    ST,
    dmid,
    DQ,
    acc,
    SP,
    SPr,
    G,
    SB,
    AG,
    RL,
    VS,
    V1,
    V2,
    nr_send,
    nr_recv,
    do_send,
    do_recv,
    st_send,
    st_recv,
    sp_send,
    sp_recv,
    red_send,
    red_recv,
    vec_send,
    vec_recv,
    out_sem,
    in_sem,
    row_sem,
):
    clips = tok.shape[0]
    rows = tok.shape[1]
    me_f = lax.axis_index("frame")
    me_c = lax.axis_index("clip")
    core, zi = lax.rem(me_c, 2), lax.div(me_c, 2)
    first, last = me_f == 0, me_f == nf - 1

    def fetch(ref, k, c):
        return pltpu.make_async_copy(ref.at[c], TI.at[c], in_sem.at[k, c])

    def put(n, ref, c):
        slot = lax.rem(n, 2)
        cp = pltpu.make_async_copy(OS.at[slot], ref.at[c], row_sem.at[slot])
        pl.when(n >= 2)(cp.wait)
        OS[slot] = low(ys[0:rows, :])
        cp.start()

    for c in range(clips):
        fetch(tok, 0, c).start()

    NR[...] = jnp.zeros(NR.shape, bf16)
    for c in range(clips):
        for s in (0, 3):
            dOT[c * 4 + s] = jnp.zeros(dOT.shape[1:], bf16)
            ST[c * 4 + s] = jnp.where(iota((3, 8, QL), 1) < 2, 1e30, 0.0)

    barrier = pltpu.get_barrier_semaphore()
    near = [
        (lax.rem(me_f + k, nf), zi * 2 + lax.rem(core + m, 2))
        for k in range(nf)
        for m in range(2)
        if k or m
    ]
    far = [(me_f, lax.rem(zi + k, nz) * 2 + core) for k in range(1, nz)]
    peers = near + far
    for peer in peers:
        pl.semaphore_signal(barrier, inc=1, device_id=peer, device_id_type=MESH)

    def halo(src, dst, send, recv, to_right):
        return pltpu.make_async_remote_copy(
            src_ref=src,
            dst_ref=dst,
            send_sem=send,
            recv_sem=recv,
            device_id=((me_f + 1) if to_right else (me_f - 1), me_c),
            device_id_type=MESH,
        )

    def nr_copy(c, right):
        i, o, k = (2, 0, 0) if right else (1, 3, 1)
        return halo(
            NR.at[c * 4 + i, pl.ds(0, KR)],
            NR.at[c * 4 + o, pl.ds(0, KR)],
            nr_send.at[c, k],
            nr_recv.at[c, k],
            right,
        )

    def do_copies(c, right):
        i, o, k = (2, 0, 0) if right else (1, 3, 1)
        return (
            halo(
                dOT.at[c * 4 + i], dOT.at[c * 4 + o], do_send.at[c, k], do_recv.at[c, k], right
            ),
            halo(ST.at[c * 4 + i], ST.at[c * 4 + o], st_send.at[c, k], st_recv.at[c, k], right),
        )

    def each_side(start, make):
        for right, here, there in ((True, last, first), (False, first, last)):

            @pl.when(jnp.logical_not(here))
            def _():
                for cp in make(right):
                    if start:
                        cp.start()
                    else:
                        cp.wait_send()

            if not start:

                @pl.when(jnp.logical_not(there))
                def _():
                    for cp in make(right):
                        cp.wait_recv()

    xs[...] = jnp.zeros(xs.shape, f32)
    mw[...] = jnp.zeros(mw.shape, f32)
    one_d = eye(D)
    one_q = eye(QL)

    def column(i):
        return wide(cb[i])

    def as_row(ref, k):
        return ref[k * D : (k + 1) * D].reshape(1, D)

    table = [(vqb, 0), (vvb, 0), (vpb, 0)] + [(vub, k) for k in range(4)]
    table += [(v, 0) for v in (vdb, vg1, vs1, vg2, vs2)]
    for i, (ref, k) in enumerate(table):
        cb[i] = jnp.transpose(jnp.broadcast_to(as_row(ref, k), (128, D)))
    n1T[...] = jnp.ones(n1T.shape, bf16)
    n2T[...] = jnp.ones(n2T.shape, bf16)
    ctxT[...] = jnp.ones(ctxT.shape, bf16)
    def frame_rows(f):
        v = xs[pl.ds(HW * f, KR), :]
        tail = jnp.where(iota((16, D), 0) < HW - (KR - 16), v[KR - 16 :], 0.0)
        return low(jnp.concatenate([v[: KR - 16], tail, jnp.zeros((QL - KR, D), f32)], axis=0))

    def norm_one(c):
        xs[0:rows, :] = TI[c].astype(f32)
        for f in range(2):
            xT = dot_t(one_d, frame_rows(f))
            XT[c * 2 + f] = low(xT)
            cent = xT - jnp.sum(xT, axis=0, keepdims=True) * (1.0 / D)
            var = jnp.sum(cent * cent, axis=0, keepdims=True) * (1.0 / D)
            nT = low(cent * lax.rsqrt(var + EPSILON) * column(G1) + column(S1))
            n1T[0:D, ds((c * 2 + f) * QL, QL, QL)] = nT
            NR[c * 4 + f + 1, 0:KR, :] = low(dot_t(one_q[0:KR], nT))

    def turn(j):
        if j < 2:
            col = (0, 2 * D)[j]
            wqvT[j * D : (j + 1) * D, :] = low(dot_t(one_d, wqkv[:, col : col + D]))
        if j == 2:
            wpT[...] = low(dot_t(one_d, wp[...]))
        wuT[j * D : (j + 1) * D, :] = low(dot_t(one_d, wu[:, j * D : (j + 1) * D]))
        wdT[:, j * D : (j + 1) * D] = low(dot_t(one_d, wd[j * D : (j + 1) * D, :]))

    fetch(tok, 0, 0).wait()
    norm_one(0)
    pl.semaphore_wait(barrier, len(peers))
    each_side(True, lambda right: (nr_copy(0, right),))
    for c in range(1, clips):
        fetch(tok, 0, c).wait()
    for n in range(1, max(clips, 5)):
        if n < clips:
            norm_one(n)
        if n < 5:
            turn(n - 1)
    for c in range(clips):
        fetch(og, 1, c).start()

    for r in (G, VS, acc):
        r[...] = jnp.zeros(r.shape, f32)
    KT[...] = jnp.zeros(KT.shape, bf16)
    SG[...] = jnp.zeros(SG.shape, bf16)

    before_bias = jnp.where(first, NEGATIVE, 0.0).astype(f32)
    after_bias = jnp.where(last, NEGATIVE, 0.0).astype(f32)
    z64 = jnp.zeros((64, QL), bf16)
    zpad = jnp.zeros((QL - KR, QL), bf16)

    def split_heads(v):
        return (
            jnp.concatenate([v[0:64], z64], axis=0),
            jnp.concatenate([z64, v[64:128]], axis=0),
        )

    def project(c, s):
        i = c * 4 + s
        own = s in (1, 2)
        t = dot_t(wqvT[...] if own else wqvT[D:, :], NR[i])
        if own:
            put_queries(i, t[0:D])
        vT = low(t[-D:] + column(VB))
        k = low(dot(NR[i, 0:KR], wqkv[:, D : 2 * D]))
        for p in range(3):
            sl = slice(p * 128, (p + 1) * 128)
            VT[s, p] = vT[sl]
            Kr[i, p] = k[:, sl]

    def put_queries(i, t):
        qT = low(low(t + column(QB)) * 0.125)
        for p in range(3):
            QT[i, p] = qT[p * 128 : (p + 1) * 128]

    def project_back(c):
        for s in range(4):
            i = c * 4 + s
            v = low(dot(NR[i, 0:KR], wqkv[:, 2 * D :]) + as_row(vvb, 0))
            for p in range(3):
                Vr[i, p] = v[:, p * 128 : (p + 1) * 128]
            if s in (0, 3):
                put_queries(i, dot_t(wqvT[0:D, :], NR[i]))

    def ss(k):
        return SS.at[k]

    def one_head(v, hh):
        return split_heads(v)[hh]

    def mask_tail(v, fill):
        tail = jnp.where(iota((16, QL), 0) < HW - (KR - 16), v[KR - 16 :], fill)
        return jnp.concatenate([v[: KR - 16], tail], axis=0)

    def forward(c):
        units = [(f, p, hh) for p in range(3) for f in range(2) for hh in range(2)]
        tops, totals, held = {}, {}, {}

        def scores(u, par):
            f, p, hh = u
            q = one_head(QT[c * 4 + f + 1, p], hh)
            tops_j = []
            for j in range(3):
                s = mask_tail(dot(Kr[c * 4 + f + j, p], q), NEGATIVE)
                if f + j == 0:
                    s = s + before_bias
                if f + j == 3:
                    s = s + after_bias
                ss(par * 4 + j)[...] = s
                tops_j.append(jnp.max(s, axis=0, keepdims=True))
                yield
            tops[u] = functools.reduce(jnp.maximum, tops_j)

        def soft(u, par):
            total = jnp.zeros((1, QL), f32)
            for j in range(3):
                e = jnp.exp(ss(par * 4 + j)[...] - tops[u])
                total += jnp.sum(e, axis=0, keepdims=True)
                SG[par, 0:KR, j * QL : (j + 1) * QL] = low(e)
                yield
            totals[u] = total
            f, p, hh = u
            ST[c * 4 + f + 1, p, hh : hh + 1, :] = tops[u] + jnp.log(total)

        def context(u, par):
            f, p, hh = u
            ctx = jnp.zeros((64, QL), f32)
            for j in range(3):
                e = SG[par, :, j * QL : (j + 1) * QL]
                ctx += dot(VT[f + j, p, hh * 64 : hh * 64 + 64, :], e)
                yield
            at = p * 128 + hh * 64
            ctxT[at : at + 64, f * QL : (f + 1) * QL] = low(ctx * (1.0 / totals[u]))

        for n in range(len(units) + 2):
            steps = []
            if n < len(units):
                steps.append(scores(units[n], n % 2))
            if 1 <= n <= len(units):
                steps.append(soft(units[n - 1], (n - 1) % 2))
            if n >= 2:
                steps.append(context(units[n - 2], n % 2))
            together(steps)

    def gelu_parts(v):
        t = 1.0 / (1.0 + (0.3275911 * 0.7071067811865476) * jnp.abs(v))
        e = jnp.exp2(v * v * (-0.5 * 1.4426950408889634))
        poly = 0.5 * 1.061405429
        poly = poly * t + 0.5 * -1.453152027
        poly = poly * t + 0.5 * 1.421413741
        poly = poly * t + 0.5 * -0.284496736
        poly = poly * t + 0.5 * 0.254829592
        h = poly * t * e
        phi = jnp.where(v >= 0, 1.0 - h, h)
        return phi, v * (e * 0.3989422804014327)

    def feed_forward(c):
        lanes = [slice(f * QL, (f + 1) * QL) for f in range(2)]
        keep = [None, None]

        def enter(f):
            xT = XT[c * 2 + f].astype(f32)
            mid = xT + (dot(wpT[...], ctxT[0:D, lanes[f]]) + column(PB))
            cent = mid - jnp.sum(mid, axis=0, keepdims=True) * (1.0 / D)
            var = jnp.sum(cent * cent, axis=0, keepdims=True) * (1.0 / D)
            r = lax.rsqrt(var + EPSILON)
            xh = cent * r
            n2T[0:D, lanes[f]] = low(xh * column(G2) + column(S2))
            dmid[c * 2 + f] = mid
            FY[f] = xh
            dy = frame_rows(f)
            dyR[lanes[f], :] = dy
            dyT[f] = low(dot_t(one_d, dy))
            keep[f] = r

        def act_at(k, f, j):
            return slice(k * 24 + f * 12 + 3 * j, k * 24 + f * 12 + 3 * j + 3)

        def products(u, par):
            f, j = u
            for k in range(2):
                rows_k = slice(k * 192, (k + 1) * 192)
                sl = slice(j * D + k * 192, j * D + (k + 1) * 192)
                bias = wide(cb[UB + j, rows_k, :])
                FX[2 * par, rows_k, :] = dot(wuT[sl, :], n2T[0:D, lanes[f]]) + bias
                yield
                FX[2 * par + 1, rows_k, :] = dot(wd[sl, :], dyT[f])
                yield

        def nonlinear(u, par):
            f, j = u
            for k in range(3):
                sl = slice(k * 128, (k + 1) * 128)
                pre = FX[2 * par, sl, :]
                phi, slope = gelu_parts(pre)
                AD[f * 12 + 3 * j + k] = low(pre * phi)
                AD[24 + f * 12 + 3 * j + k] = low(FX[2 * par + 1, sl, :] * (phi + slope))
                yield

        def leave(f):
            outT = dot(wdT[...], AD[f * 12 : f * 12 + 12].reshape(FF, QL))
            outT += dmid[c * 2 + f] + column(DB)
            dn = dot(wu[...], AD[24 + f * 12 : 36 + f * 12].reshape(FF, QL))
            return outT, dn

        def finish_frame(f, outT, dn):
            outl = low(outT)
            ys[pl.ds(HW * f, KR), :] = dot_t(one_q[0:KR], outl)
            sq = outT * outT
            out2 = low(outT - outl.astype(f32))
            sql = low(sq)
            sq2 = low(sq - sql.astype(f32))
            m = mw[...]
            if f == 1:
                m = pltpu.roll(m, 2 * QL - HW, 1)
            m = jnp.where(iota((8, QL), 1) < HW, m[:, 0:QL], 0.0)
            w = []
            for g in range(GROUPS):
                w.append(
                    sum(
                        m[v : v + 1, :] * jnp.where(grp[v, c] == g, 1.0, 0.0).astype(f32)
                        for v in range(2)
                    )
                )
            row = iota((16, QL), 0)

            def place(k):
                return jnp.where(row == k, w[0], jnp.where(row == k + 1, w[1], 0.0))

            w1, w2 = low(place(0)), low(place(2))
            cnt = jnp.sum(place(4), axis=1, keepdims=True)
            sums = dot_t(w1, outl) + dot_t(w1, out2) + dot_t(w2, sql) + dot_t(w2, sq2) + cnt
            if f == 0:
                SP[c] = sums[0:8]
            else:
                SP[c] = SP[c] + sums[0:8]
            xh = FY[f]
            acc[0] += fold(dn * xh)
            acc[1] += fold(dn)
            gg = dn * column(G2)
            m1 = jnp.sum(gg, axis=0, keepdims=True) * (1.0 / D)
            m2 = jnp.sum(gg * xh, axis=0, keepdims=True) * (1.0 / D)
            gm = dyT[f].astype(f32) + keep[f] * (gg - m1 - xh * m2)
            dmid[c * 2 + f] = gm
            ga = low(gm)
            gattT[:, lanes[f]] = ga
            gc = low(dot(wp[...], ga))
            i = c * 4 + f + 1
            prod = gc.astype(f32) * ctxT[0:D, lanes[f]].astype(f32)
            for h in range(HEADS):
                ST[i, h // 2, 2 + h % 2 : 3 + h % 2, :] = jnp.sum(
                    prod[h * 64 : h * 64 + 64], axis=0, keepdims=True
                )
            for p in range(3):
                dOT[i, p] = gc[p * 128 : (p + 1) * 128]

        def both(k, j):
            return jnp.concatenate([AD[act_at(k, f, j)].reshape(D, QL) for f in range(2)], axis=1)

        units = [(f, j) for f in range(2) for j in range(4)]
        left = {}
        enter(0)
        for n in range(len(units) + 1):
            steps = []
            if n < len(units):
                steps.append(products(units[n], n % 2))
            if n >= 1:
                steps.append(nonlinear(units[n - 1], (n - 1) % 2))
            if n == 1:
                enter(1)
            together(steps)
            if n == 5:
                left[0] = leave(0)
            if n == 6:
                finish_frame(0, *left[0])
        left[1] = leave(1)
        for j in range(4):
            G[j * D : (j + 1) * D, :] += dot(both(0, j), dyR[...])
        finish_frame(1, *left[1])
        for j in range(4):
            g = dot_t(n2T[...], both(1, j))
            G[G_UP + j * D : G_UP + (j + 1) * D, :] += g[0:D]
            VS[V_UB + j : V_UB + j + 1, :] += g[D : D + 1]
        g = dot_t(ctxT[...], gattT[...])
        G[G_PROJ:G_QKV, :] += g[0:D]
        VS[V_PB : V_PB + 1, :] += g[D : D + 1]
        VS[V_DB : V_DB + 1, :] += dot(n2T[D : D + 16, :], dyR[...])[0:1]

    def front(c, _):
        project(c, 1)
        project(c, 2)
        each_side(False, lambda right: (nr_copy(c, right),))

        @pl.when(c == 0)
        def _():
            each_side(True, lambda right: (nr_copy(1, right),))

        project(c, 0)
        project(c, 3)

        forward(c)

        @pl.when(c == 0)
        def _():
            for n in range(2, clips):
                each_side(True, lambda right: (nr_copy(n, right),))

        fetch(og, 1, c).wait()
        xs[0:rows, :] = TI[c].astype(f32)
        mw[0:2, 0:rows] = masks[c].astype(f32)
        feed_forward(c)
        each_side(True, lambda right: do_copies(c, right))
        put(c, bout, c)
        return 0

    lax.fori_loop(0, clips, front, 0)

    def gather_rows(row, k):
        VS[row : row + 1, :] = jnp.sum(jnp.transpose(acc[k]), axis=0, keepdims=True)

    gather_rows(V_G2, 0)
    gather_rows(V_S2, 1)

    me = (me_f, me_c)
    refs, red_sems = (G, SB, AG, RL), (red_send, red_recv)
    red = [Reduce(k, refs, red_sems, me, nf, nz) for k in range(len(CHUNKS))]
    for k in range(3):
        red[k].step(1)

    def sp_copies():
        return [
            pltpu.make_async_remote_copy(
                src_ref=SP,
                dst_ref=SPr.at[k - 1],
                send_sem=sp_send.at[k - 1],
                recv_sem=sp_recv.at[k - 1],
                device_id=(lax.rem(me_f + k, nf), me_c),
                device_id_type=MESH,
            )
            for k in range(1, nf)
        ]

    for cp in sp_copies():
        cp.start()

    has_before = jnp.where(first, 0.0, 1.0).astype(f32)
    has_after = jnp.where(last, 0.0, 1.0).astype(f32)

    def back_pair(c, p):
        blocks = [(0, 1), (1, 1), (2, 1), (1, 0), (1, 2), (2, 2), (3, 2), (2, 3)]
        units = [(q, g, hh) for q, g in blocks for hh in range(2)]

        def lanes_of(q, g, hh):
            k = ((q - g + 1) if g in (1, 2) else 3) * 2 + hh
            return (0 if g < 2 else 1), slice(k * QL, (k + 1) * QL)

        def products(u, par):
            q, g, hh = u
            ss(2 * par)[...] = dot(Kr[c * 4 + g, p], one_head(QT[c * 4 + q, p], hh))
            yield
            ss(2 * par + 1)[...] = dot(Vr[c * 4 + g, p], one_head(dOT[c * 4 + q, p], hh))
            yield

        def gradient(u, par):
            q, g, hh = u
            i = c * 4 + q
            side, at = lanes_of(q, g, hh)
            keep = {0: has_before, 3: has_after}.get(g)
            for lo, hi in ((0, 112), (112, KR)):
                pr = jnp.exp(ss(2 * par)[lo:hi, :] - ST[i, p, hh : hh + 1, :])
                if keep is not None:
                    pr = pr * keep
                if hi == KR:
                    tail = jnp.where(iota((16, QL), 0) < HW - (KR - 16), pr[KR - 16 - lo :], 0.0)
                    pr = jnp.concatenate([pr[: KR - 16 - lo], tail], axis=0)
                if g in (1, 2):
                    PG[side, lo:hi, at] = low(pr)
                dp = ss(2 * par + 1)[lo:hi, :] - ST[i, p, 2 + hh : 3 + hh, :]
                SG[side, lo:hi, at] = low(pr * dp)
                yield

        def keys_done(g):
            side, f = g - 1, g - 1
            qs = [c * 4 + g - 1 + k for k in range(3)]
            doms = jnp.concatenate([one_head(dOT[i, p], hh) for i in qs for hh in range(2)], axis=1)
            qms = jnp.concatenate([one_head(QT[i, p], hh) for i in qs for hh in range(2)], axis=1)
            gv = dot_t(PG[side], doms)
            gk = dot_t(SG[side, 0:KR, 0 : 6 * QL], qms)
            kv = jnp.concatenate([low(jnp.concatenate([gk, gv], axis=1)), zpad], axis=0)
            AD[pl.ds(2 * (p * 2 * clips + c * 2 + f), 2)] = kv.reshape(2, 128, QL)

        def queries_done(q):
            out = []
            for hh in range(2):
                total = jnp.zeros((64, QL), f32)
                for g in (q - 1, q, q + 1):
                    side, at = lanes_of(q, g, hh)
                    total += dot(KT[g, hh * 64 : hh * 64 + 64, :], SG[side, :, at])
                out.append(total)
            DQ[p, :, ds((c * 2 + q - 1) * QL, QL, QL)] = low(
                jnp.concatenate(out, axis=0) * 0.125
            )

        for n in range(len(units) + 1):
            steps = []
            if n < len(units):
                steps.append(products(units[n], n % 2))
            if n >= 1:
                steps.append(gradient(units[n - 1], (n - 1) % 2))
            together(steps)
            if n == 7:
                keys_done(1)
            if n == 11:
                queries_done(1)
            if n == 15:
                keys_done(2)
        queries_done(2)

    plan = {
        0: ((0, 2),),
        1: ((1, 2), (2, 2)),
        3: ((3, 1),),
        4: ((0, 3), (3, 2)),
        5: ((2, 3),),
        6: ((0, 4),),
        7: ((4, 1), (1, 3)),
        8: ((0, 5), (3, 3), (4, 2), (2, 4)),
        9: ((1, 4),),
        11: ((5, 1), (1, 5), (3, 4), (2, 5)),
        12: ((5, 2), (4, 3)),
        13: ((3, 5), (0, 6)),
        14: ((4, 4), (2, 6)),
        15: ((5, 3), (3, 6), (1, 6)),
    }
    after_vectors = (((4, 5), (5, 4), (5, 5)), ((4, 6),))

    def advance(it):
        for when_it, steps in plan.items():

            @pl.when(it == when_it)
            def _():
                for k, stage in steps:
                    red[k].step(stage)

    def qkv_grad(p):
        kv = AD[pl.ds(p * 4 * clips, 4 * clips)].reshape(2 * clips * QL, QL)
        g = jnp.concatenate([dot_t(n1T[...], DQ[p]), dot(n1T[...], kv)], axis=1)
        G[ds(G_QKV + p * D, D, D), :] = g[0:D]
        at = pl.ds(pl.multiple_of(p * 128, 128), 128)
        VS[V_QB : V_QB + 1, at] = g[D : D + 1, 0:128]
        VS[V_VB : V_VB + 1, at] = g[D : D + 1, 2 * 128 :]

    def back(it, _):
        c, p = lax.rem(it, clips), lax.div(it, clips)

        @pl.when(p == 0)
        def _():
            project_back(c)
            each_side(False, lambda right: do_copies(c, right))

        for g in range(4):
            KT[g, :, 0:KR] = low(dot_t(one_q[0:128, 0:128], Kr[c * 4 + g, p]))
        back_pair(c, p)

        @pl.when(c == clips - 1)
        def _():
            qkv_grad(p)

        advance(it)
        return 0

    lax.fori_loop(0, 3 * clips, back, 0)

    def last_norm(c, _):
        for f in range(2):
            b = c * 2 + f
            lanes = ds(b * QL, QL, QL)
            dq = jnp.concatenate([DQ[p, :, lanes] for p in range(3)], axis=0)
            kv = [AD[pl.ds(2 * (p * 2 * clips + b), 2)].reshape(QL, QL) for p in range(3)]
            dk = jnp.concatenate([v[:, 0:128] for v in kv], axis=1)
            dv = jnp.concatenate([v[:, 128:256] for v in kv], axis=1)
            dn = dot(wqkv[:, 0:D], dq) + dot_t(wqkv[:, D : 2 * D], dk)
            dn += dot_t(wqkv[:, 2 * D :], dv)
            xT = XT[b].astype(f32)
            cent = xT - jnp.sum(xT, axis=0, keepdims=True) * (1.0 / D)
            var = jnp.sum(cent * cent, axis=0, keepdims=True) * (1.0 / D)
            r = lax.rsqrt(var + EPSILON)
            xh = cent * r
            acc[2] += fold(dn * xh)
            acc[3] += fold(dn)
            gg = dn * column(G1)
            m1 = jnp.sum(gg, axis=0, keepdims=True) * (1.0 / D)
            m2 = jnp.sum(gg * xh, axis=0, keepdims=True) * (1.0 / D)
            gT = low(dmid[b] + r * (gg - m1 - xh * m2))
            ys[pl.ds(HW * f, KR), :] = dot_t(one_q[0:KR], gT)
        put(clips + c, gtok, c)
        advance(3 * clips + c)
        return 0

    lax.fori_loop(0, clips, last_norm, 0)
    gather_rows(V_G1, 2)
    gather_rows(V_S1, 3)

    def out_copy(k):
        off, n, _ = CHUNKS[k]
        rows = pl.ds(off, n)
        return pltpu.make_async_copy(AG.at[rows], out_g.at[rows], out_sem.at[k])

    def group_results():
        for cp in sp_copies():
            cp.wait()
        for c in range(clips):
            t = SP[c] + sum(SPr[k, c] for k in range(nf - 1))
            inv = 1.0 / jnp.maximum(t[4:6], 1.0)
            mean = t[0:2] * inv
            var = t[2:4] * inv - mean * mean
            stats[c, 0:1, :] = mean[0:1]
            stats[c, 1:2, :] = var[0:1]
            stats[c, 2:3, :] = mean[1:2]
            stats[c, 3:4, :] = var[1:2]

    groups = ((V1, near, 0), (V2, far, len(near)))
    for n, (dst, devs, at) in enumerate(groups):
        cps = [
            pltpu.make_async_remote_copy(
                src_ref=VS.at[pl.ds(16 * n, 16)],
                dst_ref=dst.at[k],
                send_sem=vec_send.at[at + k],
                recv_sem=vec_recv.at[at + k],
                device_id=dev,
                device_id_type=MESH,
            )
            for k, dev in enumerate(devs)
        ]
        for cp in cps:
            cp.start()
        for k, stage in after_vectors[n]:
            red[k].step(stage)
        if n == 0:
            group_results()
        for k in ((0, 3), (1, 2))[n]:
            red[k].step(7)
            out_copy(k).start()
        for cp in cps:
            cp.wait()
        total = VS[16 * n : 16 * n + 16, :]
        for k in range(len(devs)):
            total += dst[k]
        VS[16 * (n + 1) : 16 * (n + 2), :] = total
    copy_v = pltpu.make_async_copy(VS.at[pl.ds(32, 16)], out_v, out_sem.at[len(CHUNKS)])
    copy_v.start()

    red[5].step(6)
    for k in (4, 5):
        red[k].step(7)
        out_copy(k).start()
    for slot in range(2):
        pltpu.make_async_copy(OS.at[slot], gtok.at[0], row_sem.at[slot]).wait()
    for k in range(len(CHUNKS)):
        out_copy(k).wait()
    copy_v.wait()


def local(nf, nz, tokens, out_grad, view_masks, view_group, *params):
    w_qkv, query_bias, value_bias, w_proj, proj_bias, w_up, up_bias, w_down = params[:8]
    clips, rows, width = tokens.shape
    vmem = pl.BlockSpec(memory_space=pltpu.VMEM)
    hbm = pl.BlockSpec(memory_space=pl.ANY)
    sems = pltpu.SemaphoreType.DMA
    n_red = Reduce.count(nf, nz)
    _, landing = spans(nf, nz)
    bout, stats, gtok, out_g, out_v = pl.pallas_call(
        functools.partial(body, nf, nz),
        out_shape=(
            jax.ShapeDtypeStruct((clips, rows, D), bf16),
            jax.ShapeDtypeStruct((clips, 4, D), f32),
            jax.ShapeDtypeStruct((clips, rows, D), bf16),
            jax.ShapeDtypeStruct((G_ROWS, D), bf16),
            jax.ShapeDtypeStruct((16, D), f32),
        ),
        in_specs=[hbm, hbm, vmem, pl.BlockSpec(memory_space=pltpu.SMEM)] + [vmem] * 13,
        out_specs=(hbm, vmem, hbm, hbm, hbm),
        scratch_shapes=[
            pltpu.VMEM((2 * D, D), bf16),
            pltpu.VMEM((D, D), bf16),
            pltpu.VMEM((FF, D), bf16),
            pltpu.VMEM((D, FF), bf16),
            pltpu.VMEM((12, D, 128), f32),
            pltpu.VMEM((clips, rows, D), bf16),
            pltpu.VMEM((2, rows, D), bf16),
            pltpu.VMEM((408, D), f32),
            pltpu.VMEM((408, D), f32),
            pltpu.VMEM((8, 2 * QL), f32),
            pltpu.VMEM((clips * 2, D, QL), bf16),
            pltpu.VMEM((D + 16, clips * 2 * QL), bf16),
            pltpu.VMEM((clips * 4, QL, D), bf16),
            pltpu.VMEM((clips * 4, 3, 128, QL), bf16),
            pltpu.VMEM((4, 128, QL), bf16),
            pltpu.VMEM((4, 3, 128, QL), bf16),
            pltpu.VMEM((clips * 4, 3, KR, 128), bf16),
            pltpu.VMEM((clips * 4, 3, KR, 128), bf16),
            pltpu.VMEM((D + 16, 2 * QL), bf16),
            pltpu.VMEM((D + 16, 2 * QL), bf16),
            pltpu.VMEM((48, 128, QL), bf16),
            pltpu.VMEM((D, 2 * QL), bf16),
            pltpu.VMEM((2 * QL, D), bf16),
            pltpu.VMEM((clips * 4, 3, 128, QL), bf16),
            pltpu.VMEM((2, D, QL), bf16),
            pltpu.VMEM((4, D, QL), f32),
            pltpu.VMEM((2, D, QL), f32),
            pltpu.VMEM((8, KR, QL), f32),
            pltpu.VMEM((2, KR, 6 * QL), bf16),
            pltpu.VMEM((2, QL, 8 * QL), bf16),
            pltpu.VMEM((clips * 4, 3, 8, QL), f32),
            pltpu.VMEM((clips * 2, D, QL), f32),
            pltpu.VMEM((3, 128, clips * 2 * QL), bf16),
            pltpu.VMEM((4, D, 128), f32),
            pltpu.VMEM((clips, 8, D), f32),
            pltpu.VMEM((nf - 1, clips, 8, D), f32),
            pltpu.VMEM((G_ROWS, D), f32),
            pltpu.VMEM((G_ROWS, D), bf16),
            pltpu.VMEM((G_ROWS, D), bf16),
            pltpu.VMEM((landing, D), bf16),
            pltpu.VMEM((48, D), f32),
            pltpu.VMEM((2 * nf - 1, 16, D), f32),
            pltpu.VMEM((nz - 1, 16, D), f32),
            sems((clips, 2)),
            sems((clips, 2)),
            sems((clips, 2)),
            sems((clips, 2)),
            sems((clips, 2)),
            sems((clips, 2)),
            sems((nf - 1,)),
            sems((nf - 1,)),
            sems((len(CHUNKS), n_red)),
            sems((len(CHUNKS), n_red)),
            sems((2 * nf + nz - 2,)),
            sems((2 * nf + nz - 2,)),
            sems((len(CHUNKS) + 1,)),
            sems((2, clips)),
            sems((2,)),
        ],
        compiler_params=pltpu.CompilerParams(
            collective_id=0, has_side_effects=True, vmem_limit_bytes=64 * 1024 * 1024 - 65536
        ),
    )(
        tokens,
        out_grad,
        view_masks,
        view_group.T,
        w_qkv,
        w_proj,
        w_up,
        w_down,
        query_bias,
        value_bias,
        proj_bias,
        up_bias,
        *params[8:],
    )

    shape = jax.ShapeDtypeStruct
    outs = pl.pallas_call(
        finish,
        out_shape=(
            shape(bout.shape, bf16),
            shape(gtok.shape, bf16),
            shape((D, 3 * D), f32),
            shape((D, D), f32),
            shape((D, FF), f32),
            shape((FF, D), f32),
        )
        + (shape((D,), f32),) * 3
        + (shape((FF,), f32),)
        + (shape((D,), f32),) * 5
        + (shape((clips, GROUPS, 2, D), f32),),
        in_specs=[hbm] * 4 + [vmem],
        out_specs=(hbm,) * 6 + (vmem,) * 10,
        scratch_shapes=[
            pltpu.VMEM((G_ROWS, D), bf16),
            pltpu.VMEM((16, D), f32),
            pltpu.VMEM((D, 3 * D), f32),
            pltpu.VMEM((D, D), f32),
            pltpu.VMEM((D, FF), f32),
            pltpu.VMEM((FF, D), f32),
            pltpu.VMEM((2,) + bout.shape, bf16),
            sems((13,)),
            sems((12,)),
            sems((2, 2)),
        ],
        compiler_params=pltpu.CompilerParams(vmem_limit_bytes=64 * 1024 * 1024 - 65536),
    )(bout, gtok, out_g, out_v, stats)
    bout, gtok, g_qkv, g_proj, g_up, g_down, qb, vb, pb, ub, db, g1, s1, g2, s2, stats = outs
    return (bout, stats, gtok, g_qkv, qb, vb, g_proj, pb, g_up, ub, g_down, db, g1, s1, g2, s2)


def finish(
    bout_in,
    gtok_in,
    g_in,
    v_in,
    stats_in,
    bout,
    gtok,
    g_qkv,
    g_proj,
    g_up,
    g_down,
    qb,
    vb,
    pb,
    ub,
    db,
    g1,
    s1,
    g2,
    s2,
    stats,
    g,
    v,
    t_qkv,
    t_proj,
    t_up,
    t_down,
    t_rows,
    in_sem,
    out_sem,
    row_sem,
):
    rows_in = [
        pltpu.make_async_copy(src, t_rows.at[k], row_sem.at[0, k])
        for k, src in enumerate((bout_in, gtok_in))
    ]
    rows_out = [
        pltpu.make_async_copy(t_rows.at[k], dst, row_sem.at[1, k])
        for k, dst in enumerate((bout, gtok))
    ]
    loads = [
        pltpu.make_async_copy(g_in.at[pl.ds(k * D, D)], g.at[pl.ds(k * D, D)], in_sem.at[k])
        for k in range(12)
    ]
    loads.append(pltpu.make_async_copy(v_in, v, in_sem.at[12]))
    for cp in loads:
        cp.start()
    for cp in rows_in:
        cp.start()
    for c in range(stats.shape[0]):
        for k in range(GROUPS):
            stats[c, k] = stats_in[c, 2 * k : 2 * k + 2, :]
    stores = []
    for k in range(12):
        if k in (4, 8):
            rows_in[k // 8].wait()
            rows_out[k // 8].start()
        loads[k].wait()
        part = g[pl.ds(k * D, D), :].astype(f32)
        if k < 9:
            cols = pl.ds((k - 4) * D, D)
            src, dst = (
                (t_down.at[pl.ds(k * D, D)], g_down.at[pl.ds(k * D, D)])
                if k < 4
                else ((t_up.at[:, cols], g_up.at[:, cols]) if k < 8 else (t_proj, g_proj))
            )
            src[...] = part
            stores.append(pltpu.make_async_copy(src, dst, out_sem.at[k]))
            stores[-1].start()
        else:
            for j in range(3):
                at = j * D + (k - 9) * 128
                t_qkv[:, at : at + 128] = part[:, j * 128 : (j + 1) * 128]
    stores.append(pltpu.make_async_copy(t_qkv, g_qkv, out_sem.at[9]))
    stores[-1].start()
    loads[12].wait()
    for k in range(4):
        ub[k * D : (k + 1) * D] = v[V_UB + k]
    table = ((pb, V_PB), (db, V_DB), (g2, V_G2), (s2, V_S2))
    table += ((qb, V_QB), (vb, V_VB), (g1, V_G1), (s1, V_S1))
    for ref, k in table:
        ref[...] = v[k]
    for cp in stores + rows_out:
        cp.wait()


def solution(mesh):
    row = P("clip", "frame", None)
    in_specs = (row, row, P("clip", None, "frame"), P("clip", None)) + (P(),) * 13
    out_specs = (row, P("clip", None, None, None), row) + (P(),) * 13
    step = functools.partial(local, mesh.shape["frame"], mesh.shape["clip"] // 2)
    return jax.shard_map(step, mesh=mesh, in_specs=in_specs, out_specs=out_specs, check_vma=False)
```

```python
import functools

import jax
import jax.numpy as jnp
from jax import lax
from jax.experimental import pallas as pl
from jax.experimental.pallas import tpu as pltpu
from jax.sharding import PartitionSpec as P

HEADS = 6
NF = 8
HW = 196
GROUPS = 2
EPSILON = 1e-06
NEGATIVE = -1e30
MESH = pl.DeviceIdType.MESH
f32 = jnp.float32
bf16 = jnp.bfloat16

D = 384
FF = 1536
KR = 208
QL = 256
QB, VB, PB, UB, DB, G1, S1, G2, S2 = 0, 1, 2, 3, 7, 8, 9, 10, 11
G_UP, G_PROJ, G_QKV = FF, 2 * FF, 2 * FF + D
G_ROWS = G_QKV + 3 * D
CHUNKS = ((0, FF, False), (G_UP, FF, False), (G_PROJ, D, True))
CHUNKS += tuple((G_QKV + k * D, D, True) for k in range(3))
V_UB, V_PB, V_DB, V_G2, V_S2, V_QB, V_VB, V_G1, V_S1 = 0, 4, 5, 6, 7, 8, 9, 10, 11


def dot(a, b):
    return lax.dot_general(a, b, (((1,), (0,)), ((), ())), preferred_element_type=f32)


def dot_t(a, b):
    return lax.dot_general(a, b, (((1,), (1,)), ((), ())), preferred_element_type=f32)


def iota(shape, dim):
    return lax.broadcasted_iota(jnp.int32, shape, dim)


def low(v):
    return v.astype(bf16)


def wide(v):
    return jnp.concatenate([v, v], axis=1)


def fold(v):
    return v[:, 0:128] + v[:, 128:256]


def eye(n):
    return low(jnp.where(iota((n, n), 0) == iota((n, n), 1), 1.0, 0.0))


def ds(start, size, step):
    return pl.ds(pl.multiple_of(start, step), size)


def both(a, b):
    return b if a is None else a if b is None else jnp.logical_and(a, b)


def when(condition, action):
    if condition is None:
        action()
    else:
        pl.when(condition)(action)


def share(rows, n):
    return next(p for p in range(16, rows + 1, 16) if rows % p == 0 and p * n >= rows)


def spans(nf, nz):
    out, start = [], 0
    for _, rows, z_first in CHUNKS:
        n2, n3 = (nz, nf) if z_first else (nf, nz)
        part = share(rows // 2, n2)
        piece = part if z_first else share(part, n3)
        out.append((start, part, start + (n2 - 1) * part, piece))
        start += (n2 - 1) * part + (n3 - 1) * piece
    return out, start


def together(steps):
    steps = list(steps)
    while steps:
        steps = [s for s in steps if next(s, steps) is not steps]


class Reduce:
    def __init__(self, chunk, refs, sems, me, nf, nz):
        self.off, rows, self.z_first = CHUNKS[chunk]
        self.g, self.sb, self.ag, self.land = refs
        self.send, self.recv = sems[0].at[chunk], sems[1].at[chunk]
        self.f, clip = me
        self.core, self.z = lax.rem(clip, 2), lax.div(clip, 2)
        self.half = rows // 2
        self.land2, self.part, self.land3, self.piece = spans(nf, nz)[0][chunk]
        self.size = (nz, nf) if self.z_first else (nf, nz)
        n3 = self.size[1]
        self.own = (self.half // self.part, n3 if self.z_first else self.part // self.piece)
        self.pos = (self.z, self.f) if self.z_first else (self.f, self.z)
        self.base = self.off + self.core * self.half
        self.qbase = self.base + self.pos[0] * self.part
        self.pbase = self.qbase if self.z_first else self.qbase + self.pos[1] * self.piece

    def at(self, start, size, ref=None):
        return (self.ag if ref is None else ref).at[ds(start, size, 16), :]

    def landing(self, level, k):
        start, rows = ((self.land2, self.part), (self.land3, self.piece))[level]
        return self.land.at[pl.ds(start + k * rows, rows), :]

    def owns(self, level, pos=None):
        if self.own[level] == self.size[level]:
            return None
        return (self.pos[level] if pos is None else pos) < self.own[level]

    def peer(self, level, k):
        t = lax.rem(self.pos[level] + k, self.size[level])
        along_z = self.z_first == (level == 0)
        dev = (self.f, t * 2 + self.core) if along_z else (t, self.z * 2 + self.core)
        return t, dev

    def copies(self, stage):
        n2, n3 = self.size
        out = []
        if stage == 1:
            o = self.at(self.off + (1 - self.core) * self.half, self.half, self.sb)
            out = [(o, o, (self.f, self.z * 2 + 1 - self.core), 0, None, None)]
        if stage in (2, 5):
            for k in range(1, n2):
                t, dev = self.peer(0, k)
                if stage == 2:
                    src = self.at(self.base + t * self.part, self.part, self.sb)
                    dst = self.landing(0, k - 1)
                    out.append((src, dst, dev, k, self.owns(0, t), self.owns(0)))
                else:
                    s, _ = self.peer(0, n2 - k)
                    src = self.at(self.qbase, self.part)
                    sem = n2 + 2 * n3 + k - 3
                    out.append((src, src, dev, sem, self.owns(0), self.owns(0, s)))
        if stage == 3 or (stage == 4 and not self.z_first):
            for k in range(1, n3):
                t, dev = self.peer(1, k)
                if stage == 3:
                    first = self.qbase if self.z_first else self.qbase + t * self.piece
                    src = self.at(first, self.piece, self.sb)
                    sent, comes = self.owns(1, t), self.owns(1)
                    out.append((src, self.landing(1, k - 1), dev, n2 + k - 1, sent, comes))
                else:
                    s, _ = self.peer(1, n3 - k)
                    src = self.at(self.pbase, self.piece)
                    out.append((src, src, dev, n2 + n3 + k - 2, self.owns(1), self.owns(1, s)))
            part = self.owns(0)
            if part is not None:
                out = [(*c[:4], both(part, c[4]), both(part, c[5])) for c in out]
        if stage == 6:
            s = self.at(self.base, self.half)
            dev = (self.f, self.z * 2 + 1 - self.core)
            out = [(s, s, dev, 2 * n2 + 2 * n3 - 3, None, None)]
        return [
            (
                pltpu.make_async_remote_copy(
                    src_ref=s,
                    dst_ref=d,
                    send_sem=self.send.at[i],
                    recv_sem=self.recv.at[i],
                    device_id=dev,
                    device_id_type=MESH,
                ),
                sent,
                comes,
            )
            for s, d, dev, i, sent, comes in out
        ]

    def start(self, stage):
        for c, sent, _ in self.copies(stage):
            when(sent, c.start)

    def wait(self, stage):
        for c, sent, comes in self.copies(stage):
            when(comes, c.wait_recv)
            when(sent, c.wait_send)

    def step(self, stage):
        if stage > 1:
            self.wait(stage - 1)
        g, sb, ag = self.g, self.sb, self.ag
        n2, n3 = self.size
        if stage == 1:
            rows = ds(self.off + (1 - self.core) * self.half, self.half, 16)
            sb[rows, :] = low(g[rows, :])
        if stage == 2:
            rows = ds(self.base, self.half, 16)
            total = g[rows, :] + sb[rows, :].astype(f32)
            g[rows, :] = total
            sb[rows, :] = low(total)
        if stage == 3:

            def sum_part():
                rows = ds(self.qbase, self.part, 16)
                total = g[rows, :]
                for k in range(n2 - 1):
                    total += self.landing(0, k)[...].astype(f32)
                g[rows, :] = total
                sb[rows, :] = low(total)

            when(self.owns(0), sum_part)
        if stage == 4:

            def sum_piece():
                rows = ds(self.pbase, self.piece, 16)
                total = g[rows, :]
                for k in range(n3 - 1):
                    total += self.landing(1, k)[...].astype(f32)
                ag[rows, :] = low(total)

            when(both(self.owns(0), self.owns(1)), sum_piece)
        if stage < 7:
            self.start(stage)

    @staticmethod
    def count(nf, nz):
        return 2 * nf + 2 * nz - 2


def body(
    nf,
    nz,
    tok,
    og,
    masks,
    grp,
    wqkv_in,
    wp_in,
    wu_in,
    wd_in,
    vqb,
    vvb,
    vpb,
    vub,
    vdb,
    vg1,
    vs1,
    vg2,
    vs2,
    bout,
    stats,
    gtok,
    out_g,
    out_v,
    wqkv,
    wp,
    wu,
    wd,
    wqvT,
    wpT,
    wuT,
    wdT,
    cb,
    TI,
    OS,
    xs,
    ys,
    mw,
    XT,
    n1T,
    NR,
    QT,
    KT,
    VT,
    Kr,
    Vr,
    ctxT,
    n2T,
    AD,
    gattT,
    dyR,
    dOT,
    dyT,
    FX,
    FY,
    SS,
    PG,
    SG,
    ST,
    dmid,
    DQ,
    acc,
    SP,
    SPr,
    G,
    SB,
    AG,
    RL,
    VS,
    V1,
    V2,
    nr_send,
    nr_recv,
    do_send,
    do_recv,
    st_send,
    st_recv,
    sp_send,
    sp_recv,
    red_send,
    red_recv,
    vec_send,
    vec_recv,
    out_sem,
    in_sem,
    row_sem,
    weight_sem,
):
    clips = tok.shape[0]
    rows = tok.shape[1]
    me_f = lax.axis_index("frame")
    me_c = lax.axis_index("clip")
    core, zi = lax.rem(me_c, 2), lax.div(me_c, 2)
    first, last = me_f == 0, me_f == nf - 1

    def fetch(ref, k, c):
        return pltpu.make_async_copy(ref.at[c], TI.at[c], in_sem.at[k, c])

    def put(n, ref, c):
        slot = lax.rem(n, 2)
        cp = pltpu.make_async_copy(OS.at[slot], ref.at[c], row_sem.at[slot])
        pl.when(n >= 2)(cp.wait)
        OS[slot] = low(ys[0:rows, :])
        cp.start()

    for c in range(clips):
        fetch(tok, 0, c).start()
    pairs = ((wqkv_in, wqkv), (wp_in, wp), (wu_in, wu), (wd_in, wd))
    weights = [
        pltpu.make_async_copy(src, dst, weight_sem.at[k]) for k, (src, dst) in enumerate(pairs)
    ]
    for cp in weights:
        cp.start()

    NR[...] = jnp.zeros(NR.shape, bf16)
    for c in range(clips):
        for s in (0, 3):
            dOT[c * 4 + s] = jnp.zeros(dOT.shape[1:], bf16)
            ST[c * 4 + s] = jnp.where(iota((3, 8, QL), 1) < 2, 1e30, 0.0)

    barrier = pltpu.get_barrier_semaphore()
    near = [
        (lax.rem(me_f + k, nf), zi * 2 + lax.rem(core + m, 2))
        for k in range(nf)
        for m in range(2)
        if k or m
    ]
    far = [(me_f, lax.rem(zi + k, nz) * 2 + core) for k in range(1, nz)]
    peers = near + far
    for peer in peers:
        pl.semaphore_signal(barrier, inc=1, device_id=peer, device_id_type=MESH)

    def halo(src, dst, send, recv, to_right):
        return pltpu.make_async_remote_copy(
            src_ref=src,
            dst_ref=dst,
            send_sem=send,
            recv_sem=recv,
            device_id=((me_f + 1) if to_right else (me_f - 1), me_c),
            device_id_type=MESH,
        )

    def nr_copy(c, right):
        i, o, k = (2, 0, 0) if right else (1, 3, 1)
        return halo(
            NR.at[c * 4 + i, pl.ds(0, KR)],
            NR.at[c * 4 + o, pl.ds(0, KR)],
            nr_send.at[c, k],
            nr_recv.at[c, k],
            right,
        )

    def do_copies(c, right):
        i, o, k = (2, 0, 0) if right else (1, 3, 1)
        return (
            halo(
                dOT.at[c * 4 + i], dOT.at[c * 4 + o], do_send.at[c, k], do_recv.at[c, k], right
            ),
            halo(ST.at[c * 4 + i], ST.at[c * 4 + o], st_send.at[c, k], st_recv.at[c, k], right),
        )

    def each_side(start, make):
        for right, here, there in ((True, last, first), (False, first, last)):

            @pl.when(jnp.logical_not(here))
            def _():
                for cp in make(right):
                    if start:
                        cp.start()
                    else:
                        cp.wait_send()

            if not start:

                @pl.when(jnp.logical_not(there))
                def _():
                    for cp in make(right):
                        cp.wait_recv()

    xs[...] = jnp.zeros(xs.shape, f32)
    mw[...] = jnp.zeros(mw.shape, f32)
    one_d = eye(D)
    one_q = eye(QL)

    def column(i):
        return wide(cb[i])

    def as_row(ref, k):
        return ref[k * D : (k + 1) * D].reshape(1, D)

    table = [(vqb, 0), (vvb, 0), (vpb, 0)] + [(vub, k) for k in range(4)]
    table += [(v, 0) for v in (vdb, vg1, vs1, vg2, vs2)]
    for i, (ref, k) in enumerate(table):
        cb[i] = jnp.transpose(jnp.broadcast_to(as_row(ref, k), (128, D)))
    n1T[...] = jnp.ones(n1T.shape, bf16)
    n2T[...] = jnp.ones(n2T.shape, bf16)
    ctxT[...] = jnp.ones(ctxT.shape, bf16)
    def frame_rows(f):
        v = xs[pl.ds(HW * f, KR), :]
        tail = jnp.where(iota((16, D), 0) < HW - (KR - 16), v[KR - 16 :], 0.0)
        return low(jnp.concatenate([v[: KR - 16], tail, jnp.zeros((QL - KR, D), f32)], axis=0))

    def norm_one(c):
        xs[0:rows, :] = TI[c].astype(f32)
        for f in range(2):
            xT = dot_t(one_d, frame_rows(f))
            XT[c * 2 + f] = low(xT)
            cent = xT - jnp.sum(xT, axis=0, keepdims=True) * (1.0 / D)
            var = jnp.sum(cent * cent, axis=0, keepdims=True) * (1.0 / D)
            nT = low(cent * lax.rsqrt(var + EPSILON) * column(G1) + column(S1))
            n1T[0:D, ds((c * 2 + f) * QL, QL, QL)] = nT
            NR[c * 4 + f + 1, 0:KR, :] = low(dot_t(one_q[0:KR], nT))

    def turn(j):
        if j < 2:
            col = (0, 2 * D)[j]
            wqvT[j * D : (j + 1) * D, :] = low(dot_t(one_d, wqkv[:, col : col + D]))
        if j == 2:
            wpT[...] = low(dot_t(one_d, wp[...]))
        wuT[j * D : (j + 1) * D, :] = low(dot_t(one_d, wu[:, j * D : (j + 1) * D]))
        wdT[:, j * D : (j + 1) * D] = low(dot_t(one_d, wd[j * D : (j + 1) * D, :]))

    fetch(tok, 0, 0).wait()
    norm_one(0)
    pl.semaphore_wait(barrier, len(peers))
    each_side(True, lambda right: (nr_copy(0, right),))
    for c in range(1, clips):
        fetch(tok, 0, c).wait()
    for cp in weights:
        cp.wait()
    for n in range(1, max(clips, 5)):
        if n < clips:
            norm_one(n)
        if n < 5:
            turn(n - 1)
    for c in range(clips):
        fetch(og, 1, c).start()

    for r in (G, VS, acc):
        r[...] = jnp.zeros(r.shape, f32)
    KT[...] = jnp.zeros(KT.shape, bf16)
    SG[...] = jnp.zeros(SG.shape, bf16)

    before_bias = jnp.where(first, NEGATIVE, 0.0).astype(f32)
    after_bias = jnp.where(last, NEGATIVE, 0.0).astype(f32)
    z64 = jnp.zeros((64, QL), bf16)
    zpad = jnp.zeros((QL - KR, QL), bf16)

    def split_heads(v):
        return (
            jnp.concatenate([v[0:64], z64], axis=0),
            jnp.concatenate([z64, v[64:128]], axis=0),
        )

    def project(c, s):
        i = c * 4 + s
        own = s in (1, 2)
        t = dot_t(wqvT[...] if own else wqvT[D:, :], NR[i])
        if own:
            put_queries(i, t[0:D])
        vT = low(t[-D:] + column(VB))
        k = low(dot(NR[i, 0:KR], wqkv[:, D : 2 * D]))
        for p in range(3):
            sl = slice(p * 128, (p + 1) * 128)
            VT[s, p] = vT[sl]
            Kr[i, p] = k[:, sl]

    def put_queries(i, t):
        qT = low(low(t + column(QB)) * 0.125)
        for p in range(3):
            QT[i, p] = qT[p * 128 : (p + 1) * 128]

    def project_back(c):
        for s in range(4):
            i = c * 4 + s
            v = low(dot(NR[i, 0:KR], wqkv[:, 2 * D :]) + as_row(vvb, 0))
            for p in range(3):
                Vr[i, p] = v[:, p * 128 : (p + 1) * 128]
            if s in (0, 3):
                put_queries(i, dot_t(wqvT[0:D, :], NR[i]))

    def ss(k):
        return SS.at[k]

    def one_head(v, hh):
        return split_heads(v)[hh]

    def mask_tail(v, fill):
        tail = jnp.where(iota((16, QL), 0) < HW - (KR - 16), v[KR - 16 :], fill)
        return jnp.concatenate([v[: KR - 16], tail], axis=0)

    def forward(c):
        units = [(f, p, hh) for p in range(3) for f in range(2) for hh in range(2)]
        tops, totals, held = {}, {}, {}

        def scores(u, par):
            f, p, hh = u
            q = one_head(QT[c * 4 + f + 1, p], hh)
            tops_j = []
            for j in range(3):
                s = mask_tail(dot(Kr[c * 4 + f + j, p], q), NEGATIVE)
                if f + j == 0:
                    s = s + before_bias
                if f + j == 3:
                    s = s + after_bias
                ss(par * 4 + j)[...] = s
                tops_j.append(jnp.max(s, axis=0, keepdims=True))
                yield
            tops[u] = functools.reduce(jnp.maximum, tops_j)

        def soft(u, par):
            total = jnp.zeros((1, QL), f32)
            for j in range(3):
                e = jnp.exp(ss(par * 4 + j)[...] - tops[u])
                total += jnp.sum(e, axis=0, keepdims=True)
                SG[par, 0:KR, j * QL : (j + 1) * QL] = low(e)
                yield
            totals[u] = total
            f, p, hh = u
            ST[c * 4 + f + 1, p, hh : hh + 1, :] = tops[u] + jnp.log(total)

        def context(u, par):
            f, p, hh = u
            ctx = jnp.zeros((64, QL), f32)
            for j in range(3):
                e = SG[par, :, j * QL : (j + 1) * QL]
                ctx += dot(VT[f + j, p, hh * 64 : hh * 64 + 64, :], e)
                yield
            at = p * 128 + hh * 64
            ctxT[at : at + 64, f * QL : (f + 1) * QL] = low(ctx * (1.0 / totals[u]))

        for n in range(len(units) + 2):
            steps = []
            if n < len(units):
                steps.append(scores(units[n], n % 2))
            if 1 <= n <= len(units):
                steps.append(soft(units[n - 1], (n - 1) % 2))
            if n >= 2:
                steps.append(context(units[n - 2], n % 2))
            together(steps)

    def gelu_parts(v):
        t = 1.0 / (1.0 + (0.3275911 * 0.7071067811865476) * jnp.abs(v))
        e = jnp.exp2(v * v * (-0.5 * 1.4426950408889634))
        poly = 0.5 * 1.061405429
        poly = poly * t + 0.5 * -1.453152027
        poly = poly * t + 0.5 * 1.421413741
        poly = poly * t + 0.5 * -0.284496736
        poly = poly * t + 0.5 * 0.254829592
        h = poly * t * e
        phi = jnp.where(v >= 0, 1.0 - h, h)
        return phi, v * (e * 0.3989422804014327)

    def feed_forward(c):
        lanes = [slice(f * QL, (f + 1) * QL) for f in range(2)]
        keep = [None, None]

        def enter(f):
            xT = XT[c * 2 + f].astype(f32)
            mid = xT + (dot(wpT[...], ctxT[0:D, lanes[f]]) + column(PB))
            cent = mid - jnp.sum(mid, axis=0, keepdims=True) * (1.0 / D)
            var = jnp.sum(cent * cent, axis=0, keepdims=True) * (1.0 / D)
            r = lax.rsqrt(var + EPSILON)
            xh = cent * r
            n2T[0:D, lanes[f]] = low(xh * column(G2) + column(S2))
            dmid[c * 2 + f] = mid
            FY[f] = xh
            dy = frame_rows(f)
            dyR[lanes[f], :] = dy
            dyT[f] = low(dot_t(one_d, dy))
            keep[f] = r

        def act_at(k, f, j):
            return slice(k * 24 + f * 12 + 3 * j, k * 24 + f * 12 + 3 * j + 3)

        def products(u, par):
            f, j = u
            for k in range(2):
                rows_k = slice(k * 192, (k + 1) * 192)
                sl = slice(j * D + k * 192, j * D + (k + 1) * 192)
                bias = wide(cb[UB + j, rows_k, :])
                FX[2 * par, rows_k, :] = dot(wuT[sl, :], n2T[0:D, lanes[f]]) + bias
                yield
                FX[2 * par + 1, rows_k, :] = dot(wd[sl, :], dyT[f])
                yield

        def nonlinear(u, par):
            f, j = u
            for k in range(3):
                sl = slice(k * 128, (k + 1) * 128)
                pre = FX[2 * par, sl, :]
                phi, slope = gelu_parts(pre)
                AD[f * 12 + 3 * j + k] = low(pre * phi)
                AD[24 + f * 12 + 3 * j + k] = low(FX[2 * par + 1, sl, :] * (phi + slope))
                yield

        def leave(f):
            outT = dot(wdT[...], AD[f * 12 : f * 12 + 12].reshape(FF, QL))
            outT += dmid[c * 2 + f] + column(DB)
            dn = dot(wu[...], AD[24 + f * 12 : 36 + f * 12].reshape(FF, QL))
            return outT, dn

        def finish_frame(f, outT, dn):
            outl = low(outT)
            ys[pl.ds(HW * f, KR), :] = dot_t(one_q[0:KR], outl)
            sq = outT * outT
            out2 = low(outT - outl.astype(f32))
            sql = low(sq)
            sq2 = low(sq - sql.astype(f32))
            m = mw[...]
            if f == 1:
                m = pltpu.roll(m, 2 * QL - HW, 1)
            m = jnp.where(iota((8, QL), 1) < HW, m[:, 0:QL], 0.0)
            w = []
            for g in range(GROUPS):
                w.append(
                    sum(
                        m[v : v + 1, :] * jnp.where(grp[v, c] == g, 1.0, 0.0).astype(f32)
                        for v in range(2)
                    )
                )
            row = iota((16, QL), 0)

            def place(k):
                return jnp.where(row == k, w[0], jnp.where(row == k + 1, w[1], 0.0))

            w1, w2 = low(place(0)), low(place(2))
            cnt = jnp.sum(place(4), axis=1, keepdims=True)
            sums = dot_t(w1, outl) + dot_t(w1, out2) + dot_t(w2, sql) + dot_t(w2, sq2) + cnt
            if f == 0:
                SP[c] = sums[0:8]
            else:
                SP[c] = SP[c] + sums[0:8]
            xh = FY[f]
            acc[0] += fold(dn * xh)
            acc[1] += fold(dn)
            gg = dn * column(G2)
            m1 = jnp.sum(gg, axis=0, keepdims=True) * (1.0 / D)
            m2 = jnp.sum(gg * xh, axis=0, keepdims=True) * (1.0 / D)
            gm = dyT[f].astype(f32) + keep[f] * (gg - m1 - xh * m2)
            dmid[c * 2 + f] = gm
            ga = low(gm)
            gattT[:, lanes[f]] = ga
            gc = low(dot(wp[...], ga))
            i = c * 4 + f + 1
            prod = gc.astype(f32) * ctxT[0:D, lanes[f]].astype(f32)
            for h in range(HEADS):
                ST[i, h // 2, 2 + h % 2 : 3 + h % 2, :] = jnp.sum(
                    prod[h * 64 : h * 64 + 64], axis=0, keepdims=True
                )
            for p in range(3):
                dOT[i, p] = gc[p * 128 : (p + 1) * 128]

        def both(k, j):
            return jnp.concatenate([AD[act_at(k, f, j)].reshape(D, QL) for f in range(2)], axis=1)

        units = [(f, j) for f in range(2) for j in range(4)]
        left = {}
        enter(0)
        for n in range(len(units) + 1):
            steps = []
            if n < len(units):
                steps.append(products(units[n], n % 2))
            if n >= 1:
                steps.append(nonlinear(units[n - 1], (n - 1) % 2))
            if n == 1:
                enter(1)
            together(steps)
            if n == 5:
                left[0] = leave(0)
            if n == 6:
                finish_frame(0, *left[0])
        left[1] = leave(1)
        for j in range(4):
            G[j * D : (j + 1) * D, :] += dot(both(0, j), dyR[...])
        finish_frame(1, *left[1])
        for j in range(4):
            g = dot_t(n2T[...], both(1, j))
            G[G_UP + j * D : G_UP + (j + 1) * D, :] += g[0:D]
            VS[V_UB + j : V_UB + j + 1, :] += g[D : D + 1]
        g = dot_t(ctxT[...], gattT[...])
        G[G_PROJ:G_QKV, :] += g[0:D]
        VS[V_PB : V_PB + 1, :] += g[D : D + 1]
        VS[V_DB : V_DB + 1, :] += dot(n2T[D : D + 16, :], dyR[...])[0:1]

    def front(c, _):
        project(c, 1)
        project(c, 2)
        each_side(False, lambda right: (nr_copy(c, right),))

        @pl.when(c == 0)
        def _():
            each_side(True, lambda right: (nr_copy(1, right),))

        project(c, 0)
        project(c, 3)

        forward(c)

        @pl.when(c == 0)
        def _():
            for n in range(2, clips):
                each_side(True, lambda right: (nr_copy(n, right),))

        fetch(og, 1, c).wait()
        xs[0:rows, :] = TI[c].astype(f32)
        mw[0:2, 0:rows] = masks[c].astype(f32)
        feed_forward(c)
        each_side(True, lambda right: do_copies(c, right))
        put(c, bout, c)
        return 0

    lax.fori_loop(0, clips, front, 0)

    def gather_rows(row, k):
        VS[row : row + 1, :] = jnp.sum(jnp.transpose(acc[k]), axis=0, keepdims=True)

    me = (me_f, me_c)
    refs, red_sems = (G, SB, AG, RL), (red_send, red_recv)
    red = [Reduce(k, refs, red_sems, me, nf, nz) for k in range(len(CHUNKS))]
    for k in range(3):
        red[k].step(1)

    def sp_copies():
        return [
            pltpu.make_async_remote_copy(
                src_ref=SP,
                dst_ref=SPr.at[k - 1],
                send_sem=sp_send.at[k - 1],
                recv_sem=sp_recv.at[k - 1],
                device_id=(lax.rem(me_f + k, nf), me_c),
                device_id_type=MESH,
            )
            for k in range(1, nf)
        ]

    for cp in sp_copies():
        cp.start()
    gather_rows(V_G2, 0)
    gather_rows(V_S2, 1)

    has_before = jnp.where(first, 0.0, 1.0).astype(f32)
    has_after = jnp.where(last, 0.0, 1.0).astype(f32)

    def back_pair(c, p):
        blocks = [(0, 1), (1, 1), (2, 1), (1, 0), (1, 2), (2, 2), (3, 2), (2, 3)]
        units = [(q, g, hh) for q, g in blocks for hh in range(2)]

        def lanes_of(q, g, hh):
            k = ((q - g + 1) if g in (1, 2) else 3) * 2 + hh
            return (0 if g < 2 else 1), slice(k * QL, (k + 1) * QL)

        def products(u, par):
            q, g, hh = u
            ss(2 * par)[...] = dot(Kr[c * 4 + g, p], one_head(QT[c * 4 + q, p], hh))
            yield
            ss(2 * par + 1)[...] = dot(Vr[c * 4 + g, p], one_head(dOT[c * 4 + q, p], hh))
            yield

        def gradient(u, par):
            q, g, hh = u
            i = c * 4 + q
            side, at = lanes_of(q, g, hh)
            keep = {0: has_before, 3: has_after}.get(g)
            for lo, hi in ((0, 112), (112, KR)):
                pr = jnp.exp(ss(2 * par)[lo:hi, :] - ST[i, p, hh : hh + 1, :])
                if keep is not None:
                    pr = pr * keep
                if hi == KR:
                    tail = jnp.where(iota((16, QL), 0) < HW - (KR - 16), pr[KR - 16 - lo :], 0.0)
                    pr = jnp.concatenate([pr[: KR - 16 - lo], tail], axis=0)
                if g in (1, 2):
                    PG[side, lo:hi, at] = low(pr)
                dp = ss(2 * par + 1)[lo:hi, :] - ST[i, p, 2 + hh : 3 + hh, :]
                SG[side, lo:hi, at] = low(pr * dp)
                yield

        def keys_done(g):
            side, f = g - 1, g - 1
            qs = [c * 4 + g - 1 + k for k in range(3)]
            doms = jnp.concatenate([one_head(dOT[i, p], hh) for i in qs for hh in range(2)], axis=1)
            qms = jnp.concatenate([one_head(QT[i, p], hh) for i in qs for hh in range(2)], axis=1)
            gv = dot_t(PG[side], doms)
            gk = dot_t(SG[side, 0:KR, 0 : 6 * QL], qms)
            kv = jnp.concatenate([low(jnp.concatenate([gk, gv], axis=1)), zpad], axis=0)
            AD[pl.ds(2 * (p * 2 * clips + c * 2 + f), 2)] = kv.reshape(2, 128, QL)

        def queries_done(q):
            out = []
            for hh in range(2):
                total = jnp.zeros((64, QL), f32)
                for g in (q - 1, q, q + 1):
                    side, at = lanes_of(q, g, hh)
                    total += dot(KT[g, hh * 64 : hh * 64 + 64, :], SG[side, :, at])
                out.append(total)
            DQ[p, :, ds((c * 2 + q - 1) * QL, QL, QL)] = low(
                jnp.concatenate(out, axis=0) * 0.125
            )

        for n in range(len(units) + 1):
            steps = []
            if n < len(units):
                steps.append(products(units[n], n % 2))
            if n >= 1:
                steps.append(gradient(units[n - 1], (n - 1) % 2))
            together(steps)
            if n == 7:
                keys_done(1)
            if n == 11:
                queries_done(1)
            if n == 15:
                keys_done(2)
        queries_done(2)

    plan = {
        0: ((0, 2),),
        1: ((1, 2), (2, 2)),
        3: ((3, 1),),
        4: ((0, 3), (3, 2)),
        5: ((2, 3),),
        6: ((0, 4),),
        7: ((4, 1), (1, 3)),
        8: ((0, 5), (3, 3), (4, 2), (2, 4)),
        9: ((1, 4),),
        11: ((5, 1), (1, 5), (3, 4), (2, 5)),
        12: ((5, 2), (4, 3)),
        13: ((3, 5), (0, 6)),
        14: ((4, 4), (2, 6)),
        15: ((5, 3), (3, 6), (1, 6)),
    }
    after_vectors = (((4, 5), (5, 4), (5, 5)), ((4, 6),))

    def advance(it):
        for when_it, steps in plan.items():

            @pl.when(it == when_it)
            def _():
                for k, stage in steps:
                    red[k].step(stage)

    def qkv_grad(p):
        kv = AD[pl.ds(p * 4 * clips, 4 * clips)].reshape(2 * clips * QL, QL)
        g = jnp.concatenate([dot_t(n1T[...], DQ[p]), dot(n1T[...], kv)], axis=1)
        G[ds(G_QKV + p * D, D, D), :] = g[0:D]
        at = pl.ds(pl.multiple_of(p * 128, 128), 128)
        VS[V_QB : V_QB + 1, at] = g[D : D + 1, 0:128]
        VS[V_VB : V_VB + 1, at] = g[D : D + 1, 2 * 128 :]

    def back(it, _):
        c, p = lax.rem(it, clips), lax.div(it, clips)

        @pl.when(p == 0)
        def _():
            project_back(c)
            each_side(False, lambda right: do_copies(c, right))

        for g in range(4):
            KT[g, :, 0:KR] = low(dot_t(one_q[0:128, 0:128], Kr[c * 4 + g, p]))
        back_pair(c, p)

        @pl.when(c == clips - 1)
        def _():
            qkv_grad(p)

        advance(it)
        return 0

    lax.fori_loop(0, 3 * clips, back, 0)

    def last_norm(c, _):
        for f in range(2):
            b = c * 2 + f
            lanes = ds(b * QL, QL, QL)
            dq = jnp.concatenate([DQ[p, :, lanes] for p in range(3)], axis=0)
            kv = [AD[pl.ds(2 * (p * 2 * clips + b), 2)].reshape(QL, QL) for p in range(3)]
            dk = jnp.concatenate([v[:, 0:128] for v in kv], axis=1)
            dv = jnp.concatenate([v[:, 128:256] for v in kv], axis=1)
            dn = dot(wqkv[:, 0:D], dq) + dot_t(wqkv[:, D : 2 * D], dk)
            dn += dot_t(wqkv[:, 2 * D :], dv)
            xT = XT[b].astype(f32)
            cent = xT - jnp.sum(xT, axis=0, keepdims=True) * (1.0 / D)
            var = jnp.sum(cent * cent, axis=0, keepdims=True) * (1.0 / D)
            r = lax.rsqrt(var + EPSILON)
            xh = cent * r
            acc[2] += fold(dn * xh)
            acc[3] += fold(dn)
            gg = dn * column(G1)
            m1 = jnp.sum(gg, axis=0, keepdims=True) * (1.0 / D)
            m2 = jnp.sum(gg * xh, axis=0, keepdims=True) * (1.0 / D)
            gT = low(dmid[b] + r * (gg - m1 - xh * m2))
            ys[pl.ds(HW * f, KR), :] = dot_t(one_q[0:KR], gT)
        put(clips + c, gtok, c)
        advance(3 * clips + c)
        return 0

    lax.fori_loop(0, clips, last_norm, 0)
    gather_rows(V_G1, 2)
    gather_rows(V_S1, 3)

    def out_copy(k):
        off, n, _ = CHUNKS[k]
        rows = pl.ds(off, n)
        return pltpu.make_async_copy(AG.at[rows], out_g.at[rows], out_sem.at[k])

    def group_results():
        for cp in sp_copies():
            cp.wait()
        for c in range(clips):
            t = SP[c] + sum(SPr[k, c] for k in range(nf - 1))
            inv = 1.0 / jnp.maximum(t[4:6], 1.0)
            mean = t[0:2] * inv
            var = t[2:4] * inv - mean * mean
            stats[c, 0:1, :] = mean[0:1]
            stats[c, 1:2, :] = var[0:1]
            stats[c, 2:3, :] = mean[1:2]
            stats[c, 3:4, :] = var[1:2]

    groups = ((V1, near, 0), (V2, far, len(near)))
    for n, (dst, devs, at) in enumerate(groups):
        cps = [
            pltpu.make_async_remote_copy(
                src_ref=VS.at[pl.ds(16 * n, 16)],
                dst_ref=dst.at[k],
                send_sem=vec_send.at[at + k],
                recv_sem=vec_recv.at[at + k],
                device_id=dev,
                device_id_type=MESH,
            )
            for k, dev in enumerate(devs)
        ]
        for cp in cps:
            cp.start()
        for k, stage in after_vectors[n]:
            red[k].step(stage)
        if n == 0:
            group_results()
        for k in ((0, 3), (1, 2))[n]:
            red[k].step(7)
            out_copy(k).start()
        for cp in cps:
            cp.wait()
        total = VS[16 * n : 16 * n + 16, :]
        for k in range(len(devs)):
            total += dst[k]
        VS[16 * (n + 1) : 16 * (n + 2), :] = total
    copy_v = pltpu.make_async_copy(VS.at[pl.ds(32, 16)], out_v, out_sem.at[len(CHUNKS)])
    copy_v.start()

    red[5].step(6)
    for k in (4, 5):
        red[k].step(7)
        out_copy(k).start()
    for slot in range(2):
        pltpu.make_async_copy(OS.at[slot], gtok.at[0], row_sem.at[slot]).wait()
    for k in range(len(CHUNKS)):
        out_copy(k).wait()
    copy_v.wait()


def local(nf, nz, tokens, out_grad, view_masks, view_group, *params):
    w_qkv, query_bias, value_bias, w_proj, proj_bias, w_up, up_bias, w_down = params[:8]
    clips, rows, width = tokens.shape
    vmem = pl.BlockSpec(memory_space=pltpu.VMEM)
    hbm = pl.BlockSpec(memory_space=pl.ANY)
    sems = pltpu.SemaphoreType.DMA
    n_red = Reduce.count(nf, nz)
    _, landing = spans(nf, nz)
    bout, stats, gtok, out_g, out_v = pl.pallas_call(
        functools.partial(body, nf, nz),
        out_shape=(
            jax.ShapeDtypeStruct((clips, rows, D), bf16),
            jax.ShapeDtypeStruct((clips, 4, D), f32),
            jax.ShapeDtypeStruct((clips, rows, D), bf16),
            jax.ShapeDtypeStruct((G_ROWS, D), bf16),
            jax.ShapeDtypeStruct((16, D), f32),
        ),
        in_specs=[hbm, hbm, vmem, pl.BlockSpec(memory_space=pltpu.SMEM)] + [hbm] * 4 + [vmem] * 9,
        out_specs=(hbm, vmem, hbm, hbm, hbm),
        scratch_shapes=[
            pltpu.VMEM((D, 3 * D), bf16),
            pltpu.VMEM((D, D), bf16),
            pltpu.VMEM((D, FF), bf16),
            pltpu.VMEM((FF, D), bf16),
            pltpu.VMEM((2 * D, D), bf16),
            pltpu.VMEM((D, D), bf16),
            pltpu.VMEM((FF, D), bf16),
            pltpu.VMEM((D, FF), bf16),
            pltpu.VMEM((12, D, 128), f32),
            pltpu.VMEM((clips, rows, D), bf16),
            pltpu.VMEM((2, rows, D), bf16),
            pltpu.VMEM((408, D), f32),
            pltpu.VMEM((408, D), f32),
            pltpu.VMEM((8, 2 * QL), f32),
            pltpu.VMEM((clips * 2, D, QL), bf16),
            pltpu.VMEM((D + 16, clips * 2 * QL), bf16),
            pltpu.VMEM((clips * 4, QL, D), bf16),
            pltpu.VMEM((clips * 4, 3, 128, QL), bf16),
            pltpu.VMEM((4, 128, QL), bf16),
            pltpu.VMEM((4, 3, 128, QL), bf16),
            pltpu.VMEM((clips * 4, 3, KR, 128), bf16),
            pltpu.VMEM((clips * 4, 3, KR, 128), bf16),
            pltpu.VMEM((D + 16, 2 * QL), bf16),
            pltpu.VMEM((D + 16, 2 * QL), bf16),
            pltpu.VMEM((48, 128, QL), bf16),
            pltpu.VMEM((D, 2 * QL), bf16),
            pltpu.VMEM((2 * QL, D), bf16),
            pltpu.VMEM((clips * 4, 3, 128, QL), bf16),
            pltpu.VMEM((2, D, QL), bf16),
            pltpu.VMEM((4, D, QL), f32),
            pltpu.VMEM((2, D, QL), f32),
            pltpu.VMEM((8, KR, QL), f32),
            pltpu.VMEM((2, KR, 6 * QL), bf16),
            pltpu.VMEM((2, QL, 8 * QL), bf16),
            pltpu.VMEM((clips * 4, 3, 8, QL), f32),
            pltpu.VMEM((clips * 2, D, QL), f32),
            pltpu.VMEM((3, 128, clips * 2 * QL), bf16),
            pltpu.VMEM((4, D, 128), f32),
            pltpu.VMEM((clips, 8, D), f32),
            pltpu.VMEM((nf - 1, clips, 8, D), f32),
            pltpu.VMEM((G_ROWS, D), f32),
            pltpu.VMEM((G_ROWS, D), bf16),
            pltpu.VMEM((G_ROWS, D), bf16),
            pltpu.VMEM((landing, D), bf16),
            pltpu.VMEM((48, D), f32),
            pltpu.VMEM((2 * nf - 1, 16, D), f32),
            pltpu.VMEM((nz - 1, 16, D), f32),
            sems((clips, 2)),
            sems((clips, 2)),
            sems((clips, 2)),
            sems((clips, 2)),
            sems((clips, 2)),
            sems((clips, 2)),
            sems((nf - 1,)),
            sems((nf - 1,)),
            sems((len(CHUNKS), n_red)),
            sems((len(CHUNKS), n_red)),
            sems((2 * nf + nz - 2,)),
            sems((2 * nf + nz - 2,)),
            sems((len(CHUNKS) + 1,)),
            sems((2, clips)),
            sems((2,)),
            sems((4,)),
        ],
        compiler_params=pltpu.CompilerParams(
            collective_id=0, has_side_effects=True, vmem_limit_bytes=64 * 1024 * 1024 - 65536
        ),
    )(
        tokens,
        out_grad,
        view_masks,
        view_group.T,
        w_qkv,
        w_proj,
        w_up,
        w_down,
        query_bias,
        value_bias,
        proj_bias,
        up_bias,
        *params[8:],
    )

    shape = jax.ShapeDtypeStruct
    outs = pl.pallas_call(
        finish,
        out_shape=(
            shape(bout.shape, bf16),
            shape(gtok.shape, bf16),
            shape((D, 3 * D), f32),
            shape((D, D), f32),
            shape((D, FF), f32),
            shape((FF, D), f32),
        )
        + (shape((D,), f32),) * 3
        + (shape((FF,), f32),)
        + (shape((D,), f32),) * 5
        + (shape((clips, GROUPS, 2, D), f32),),
        in_specs=[hbm] * 4 + [vmem],
        out_specs=(hbm,) * 6 + (vmem,) * 10,
        scratch_shapes=[
            pltpu.VMEM((G_ROWS, D), bf16),
            pltpu.VMEM((16, D), f32),
            pltpu.VMEM((D, 3 * D), f32),
            pltpu.VMEM((D, D), f32),
            pltpu.VMEM((D, FF), f32),
            pltpu.VMEM((FF, D), f32),
            pltpu.VMEM((2,) + bout.shape, bf16),
            sems((13,)),
            sems((12,)),
            sems((2, 2)),
        ],
        compiler_params=pltpu.CompilerParams(vmem_limit_bytes=64 * 1024 * 1024 - 65536),
    )(bout, gtok, out_g, out_v, stats)
    bout, gtok, g_qkv, g_proj, g_up, g_down, qb, vb, pb, ub, db, g1, s1, g2, s2, stats = outs
    return (bout, stats, gtok, g_qkv, qb, vb, g_proj, pb, g_up, ub, g_down, db, g1, s1, g2, s2)


def finish(
    bout_in,
    gtok_in,
    g_in,
    v_in,
    stats_in,
    bout,
    gtok,
    g_qkv,
    g_proj,
    g_up,
    g_down,
    qb,
    vb,
    pb,
    ub,
    db,
    g1,
    s1,
    g2,
    s2,
    stats,
    g,
    v,
    t_qkv,
    t_proj,
    t_up,
    t_down,
    t_rows,
    in_sem,
    out_sem,
    row_sem,
):
    rows_in = [
        pltpu.make_async_copy(src, t_rows.at[k], row_sem.at[0, k])
        for k, src in enumerate((bout_in, gtok_in))
    ]
    rows_out = [
        pltpu.make_async_copy(t_rows.at[k], dst, row_sem.at[1, k])
        for k, dst in enumerate((bout, gtok))
    ]
    loads = [
        pltpu.make_async_copy(g_in.at[pl.ds(k * D, D)], g.at[pl.ds(k * D, D)], in_sem.at[k])
        for k in range(12)
    ]
    loads.append(pltpu.make_async_copy(v_in, v, in_sem.at[12]))
    for cp in loads:
        cp.start()
    for cp in rows_in:
        cp.start()
    for c in range(stats.shape[0]):
        for k in range(GROUPS):
            stats[c, k] = stats_in[c, 2 * k : 2 * k + 2, :]
    stores = []
    for k in range(12):
        if k in (4, 8):
            rows_in[k // 8].wait()
            rows_out[k // 8].start()
        loads[k].wait()
        part = g[pl.ds(k * D, D), :].astype(f32)
        if k < 9:
            cols = pl.ds((k - 4) * D, D)
            src, dst = (
                (t_down.at[pl.ds(k * D, D)], g_down.at[pl.ds(k * D, D)])
                if k < 4
                else ((t_up.at[:, cols], g_up.at[:, cols]) if k < 8 else (t_proj, g_proj))
            )
            src[...] = part
            stores.append(pltpu.make_async_copy(src, dst, out_sem.at[k]))
            stores[-1].start()
        else:
            for j in range(3):
                at = j * D + (k - 9) * 128
                t_qkv[:, at : at + 128] = part[:, j * 128 : (j + 1) * 128]
    stores.append(pltpu.make_async_copy(t_qkv, g_qkv, out_sem.at[9]))
    stores[-1].start()
    loads[12].wait()
    for k in range(4):
        ub[k * D : (k + 1) * D] = v[V_UB + k]
    table = ((pb, V_PB), (db, V_DB), (g2, V_G2), (s2, V_S2))
    table += ((qb, V_QB), (vb, V_VB), (g1, V_G1), (s1, V_S1))
    for ref, k in table:
        ref[...] = v[k]
    for cp in stores + rows_out:
        cp.wait()


def solution(mesh):
    row = P("clip", "frame", None)
    in_specs = (row, row, P("clip", None, "frame"), P("clip", None)) + (P(),) * 13
    out_specs = (row, P("clip", None, None, None), row) + (P(),) * 13
    step = functools.partial(local, mesh.shape["frame"], mesh.shape["clip"] // 2)
    return jax.shard_map(step, mesh=mesh, in_specs=in_specs, out_specs=out_specs, check_vma=False)
```
